512 devices in a mesh: span: 32 (over x, y), seq: 16 (over z, core).
Axes of the slice: x: 4, y: 8, z: 8, core: 2. Of those that a mesh axis runs over, the one named last changes fastest.
Arguments:
- q_tok: bfloat16 [65536, 2048], P(('span', 'seq')), may hold values from -300 to 300
- keys: bfloat16 [65536, 512], P(('span', 'seq')), may hold values from -6 to 6
- values: bfloat16 [65536, 512], P(('span', 'seq')), may hold values from -6 to 6
- beacon_q: bfloat16 [8192, 2048], P(('span', 'seq')), may hold values from -15 to 15
- beacon_k: bfloat16 [8192, 512], P(('span', 'seq')), may hold values from -5 to 5
- beacon_v: bfloat16 [8192, 512], P(('span', 'seq')), may hold values from -6 to 6
- beacon_pos: int32 [8192], P('span'), may hold values from 0 to 2047, as said below
- visible: int32 [32, 32], replicated, may hold values 0 or 1
Outputs:
- out_tok: bfloat16 [65536, 2048], P(('span', 'seq'))
- out_beacon: bfloat16 [8192, 2048], P(('span', 'seq'))
The draws below stay inside these ranges and needn't reach their ends.
Inputs may be any that keep to these rules, and one draw needn't show every extreme that they name: `beacon_pos`: beacon b of a span stands after raw token 8 * b + r of that span, r from 0 to 7; the first beacon of every span at 0, the last at 2047.
All inputs are finite; a program needn't handle non-finite values.
Results may differ from the reference program's by a relative error of at most 0.005.
Values may be sent and summed in bfloat16 or wider, within the bound.
No kernel may reach another device: no remote copies, remote signals or barrier semaphores. Data moves between devices by JAX's collectives and lax.ppermute only.
A program may use at most 64 MiB of HBM per device.

```python
import jax
import jax.numpy as jnp
from jax import lax

HD = 128
KVH = 4
QH = 16
RATIO = 8
SPAN = 2048
BEACONS = 256
SPANS = 32


def shared_keys(key):
    drawn = jax.random.normal(jax.random.fold_in(key, 101), (SPANS, SPAN, KVH * HD), jnp.float32)
    drawn = jnp.clip(drawn, -5.0, 5.0)
    blended = drawn[:, 5]
    return drawn.at[:, 5].set(blended)


def draw_keys(key, part):
    drawn = shared_keys(key)
    return drawn.reshape(SPANS * SPAN, KVH * HD).astype(jnp.bfloat16)


def draw_q_tok(key, part):
    key = jax.random.fold_in(key, 2)
    drawn = jnp.clip(2.5 * jax.random.normal(key, (SPANS, SPAN, QH * HD), jnp.float32), -15.0, 15.0)
    return drawn.reshape(SPANS * SPAN, QH * HD).astype(jnp.bfloat16)


def draw_beacon_pos(key, part):
    key = jax.random.fold_in(key, 3)
    offsets = jax.random.randint(key, (SPANS, BEACONS), 0, RATIO, dtype=jnp.int32)
    offsets = offsets.at[:, 0].set(0).at[:, BEACONS - 1].set(RATIO - 1)
    spacing = RATIO * jnp.arange(BEACONS, dtype=jnp.int32)
    return (spacing[None, :] + offsets).reshape(SPANS * BEACONS).astype(jnp.int32)


def touch_ends(entries, rng, low, high):
    longest = entries.shape.index(max(entries.shape))
    spots = []
    for shift in (0, 1):
        where = [jax.random.randint(jax.random.fold_in(rng, axis), (), 0, length) for axis, length in enumerate(entries.shape)]
        where[longest] = (where[longest] + shift) % entries.shape[longest]
        spots.append(tuple(where))
    return entries.at[spots[0]].set(low).at[spots[1]].set(high)


def block_levels(key, shape, cuts, low, largest):
    factor_of, own = 1.0, jax.random.fold_in(key, 6)
    for axis_at, shards_of in cuts:
        draws = jnp.exp(jax.random.uniform(jax.random.fold_in(own, axis_at), (shards_of,), jnp.float32, low / len(cuts), largest / len(cuts)))
        factor_of = factor_of * jnp.repeat(draws, shape[axis_at] // shards_of).reshape([-1 if axis == axis_at else 1 for axis in range(len(shape))])
    return factor_of


def centred(rng, shape, deviation, limit, pieces=(), kind=jnp.bfloat16):
    gain = block_levels(rng, shape, pieces, -0.22, 0.18) if pieces else 1.0
    entries = jax.random.normal(rng, shape, jnp.float32) * deviation * gain
    return jnp.minimum(jnp.maximum(entries, -limit), limit).astype(kind)


def setup_inputs(seed: int = 0) -> dict:
    streams_of = jax.random.split(jax.random.key(seed), 9)
    q_tok = draw_q_tok(jax.random.fold_in(streams_of[8], 71), 0)
    keys = draw_keys(jax.random.fold_in(streams_of[8], 71), 0)
    values = centred(streams_of[2], (SPANS * SPAN, KVH * HD), 1.0, 6.0, ((0, 512),))
    beacon_q = centred(streams_of[3], (SPANS * BEACONS, QH * HD), 2.5, 15.0, ((0, 512),))
    beacon_k = centred(streams_of[4], (SPANS * BEACONS, KVH * HD), 1.0, 5.0, ((0, 512),))
    beacon_v = centred(streams_of[5], (SPANS * BEACONS, KVH * HD), 1.0, 6.0, ((0, 512),))
    beacon_pos = draw_beacon_pos(jax.random.fold_in(streams_of[8], 71), 0)
    visible = touch_ends((jax.random.randint(streams_of[7], (SPANS, SPANS), 0, 4) < 3).astype(jnp.int32), jax.random.fold_in(streams_of[7], 1), 0, 1)
    return dict(q_tok=q_tok, keys=keys, values=values, beacon_q=beacon_q, beacon_k=beacon_k, beacon_v=beacon_v, beacon_pos=beacon_pos, visible=visible)


masked_score = -1e30


def reference(q_tok, keys, values, beacon_q, beacon_k, beacon_v, beacon_pos, visible):
    group_size = QH // KVH
    temper = HD ** -0.5
    tok_queries = q_tok.reshape(SPANS, SPAN, QH, HD)
    bea_queries = beacon_q.reshape(SPANS, BEACONS, QH, HD)
    tok_keys = keys.reshape(SPANS, SPAN, KVH, HD)
    tok_values = values.reshape(SPANS, SPAN, KVH, HD)
    bea_keys = beacon_k.reshape(SPANS, BEACONS, KVH, HD)
    bea_values = beacon_v.reshape(SPANS, BEACONS, KVH, HD)
    every_bkey = beacon_k.reshape(SPANS * BEACONS, KVH, HD)
    every_bval = beacon_v.reshape(SPANS * BEACONS, KVH, HD)
    owners = jnp.arange(SPANS * BEACONS, dtype=jnp.int32) // BEACONS
    placed = beacon_pos.reshape(SPANS, BEACONS)

    def one_span(span_id):
        asked = jnp.concatenate([tok_queries[span_id], bea_queries[span_id]], axis=0)
        key_set = jnp.concatenate([tok_keys[span_id], bea_keys[span_id], every_bkey], axis=0)
        value_set = jnp.concatenate([tok_values[span_id], bea_values[span_id], every_bval], axis=0)
        where_at = jnp.concatenate([jnp.arange(SPAN, dtype=jnp.int32), placed[span_id]])
        beacon_rank = jnp.concatenate([jnp.full((SPAN,), -1, jnp.int32), jnp.arange(BEACONS, dtype=jnp.int32)])
        see_raw = jnp.arange(SPAN, dtype=jnp.int32)[None, :] <= where_at[:, None]
        see_own = jnp.arange(BEACONS, dtype=jnp.int32)[None, :] <= beacon_rank[:, None]
        see_prior = (owners < span_id) & (visible[span_id][owners] > 0)
        allowed = jnp.concatenate([see_raw, see_own, jnp.broadcast_to(see_prior[None, :], (SPAN + BEACONS, SPANS * BEACONS))], axis=1)

        def one_head(head_id):
            kv_head = head_id // group_size
            query_h = lax.dynamic_index_in_dim(asked, head_id, 1, keepdims=False)
            key_h = lax.dynamic_index_in_dim(key_set, kv_head, 1, keepdims=False)
            value_h = lax.dynamic_index_in_dim(value_set, kv_head, 1, keepdims=False)
            scores = jnp.dot(query_h, key_h.T, preferred_element_type=jnp.float32) * temper
            scores = jnp.where(allowed, scores, masked_score)
            row_max = jnp.max(scores, axis=1, keepdims=True)
            weights = jnp.where(allowed, jnp.exp(scores - row_max), 0.0)
            total = jnp.sum(weights, axis=1, keepdims=True)
            mixed = jnp.dot(weights.astype(jnp.bfloat16), value_h, preferred_element_type=jnp.float32)
            return (mixed / total).astype(jnp.bfloat16)

        heads_out = lax.map(one_head, jnp.arange(QH, dtype=jnp.int32))
        return jnp.transpose(heads_out, (1, 0, 2)).reshape(SPAN + BEACONS, QH * HD)

    results = lax.map(one_span, jnp.arange(SPANS, dtype=jnp.int32))
    out_tok = results[:, :SPAN].reshape(SPANS * SPAN, QH * HD)
    out_beacon = results[:, SPAN:].reshape(SPANS * BEACONS, QH * HD)
    return out_tok, out_beacon
```

```python
import functools

import jax
import jax.numpy as jnp
from jax import lax
from jax.experimental import pallas as pl
from jax.experimental.pallas import tpu as pltpu
from jax.sharding import Mesh, PartitionSpec as P

HD = 128
KVH = 4
QH = 16
GROUP = QH // KVH
NX, NY, NZ, NC = 4, 8, 8, 2
TOK = 128
BEA = 16
HEAD_ROWS = TOK + BEA
TILE = GROUP * HEAD_ROWS
TILES = 4
ROWS = TILES * TILE
HALF = 128
SCALE = HD**-0.5 * 1.4426950408889634
LOWEST = -1e30
CHIPS = ("x", "y", "z", "core")
CONTRACT_LAST = (((1,), (1,)), ((), ()))
VMEM = pl.BlockSpec(memory_space=pltpu.VMEM)
SMEM = pl.BlockSpec(memory_space=pltpu.SMEM)
BF16 = jnp.bfloat16
F32 = jnp.float32


def moves(target):
    pairs = []
    for x in range(NX):
        for y in range(NY):
            for z in range(NZ):
                for core in range(NC):
                    to = target(x, y, z, core)
                    if to is not None:
                        tx, ty, tz, tc = to
                        source = ((x * NY + y) * NZ + z) * NC + core
                        pairs.append((source, ((tx * NY + ty) * NZ + tz % NZ) * NC + tc))
    return pairs


def to_head_group(step):
    return moves(lambda x, y, z, core: (x, y, z + 2 * step, core))


def to_later_x(step):
    return moves(lambda x, y, z, core: (x + step, y, z, core) if x + step < NX else None)


OTHER_CORE = moves(lambda x, y, z, core: (x, y, z, 1 - core))
OTHER_PARITY = moves(lambda x, y, z, core: (x, y, z ^ 1, core))


def kernel_call(body, name, out_shape, in_specs, scratch=(), flops=0, byte_count=0):
    return pl.pallas_call(
        body,
        name=name,
        out_shape=out_shape,
        in_specs=in_specs,
        out_specs=jax.tree.map(lambda _: VMEM, out_shape),
        scratch_shapes=list(scratch),
        compiler_params=pltpu.CompilerParams(vmem_limit_bytes=48 * 2**20),
        cost_estimate=pl.CostEstimate(
            flops=flops, bytes_accessed=byte_count, transcendentals=0
        ),
    )


def pack_beacons(k_ref, v_ref, out_ref):
    for z in range(NZ):
        g = z // 2
        piece = jnp.concatenate(
            [k_ref[:, g * HD : (g + 1) * HD], v_ref[:, g * HD : (g + 1) * HD]], axis=1
        )
        for y in range(NY):
            out_ref[y * NZ + z] = piece


def pack_tokens(place, q_ref, k_ref, v_ref, bq_ref, *outs):
    g = place[2] // 2
    for step in range(TILES):
        dest = lax.rem(g + step, KVH)
        out = outs[step]
        for h in range(GROUP):
            column = pl.multiple_of((dest * GROUP + h) * HD, HD)
            out[h * HEAD_ROWS : h * HEAD_ROWS + TOK, :] = q_ref[:, pl.ds(column, HD)]
            out[h * HEAD_ROWS + TOK : (h + 1) * HEAD_ROWS, :] = bq_ref[:, pl.ds(column, HD)]
        column = pl.multiple_of(dest * HD, HD)
        out[TILE : TILE + TOK, :] = k_ref[:, pl.ds(column, HD)]
        out[TILE + TOK : TILE + 2 * TOK, :] = v_ref[:, pl.ds(column, HD)]


def absorb(state, rows, scores, values, fresh):
    m_ref, l_ref, a_ref = state
    ones = jnp.ones_like(values)
    block_max = jnp.max(scores, axis=1, keepdims=True)
    if fresh:
        new = jnp.broadcast_to(block_max, (scores.shape[0], HD))
    else:
        old = m_ref[rows, :]
        new = jnp.maximum(old, block_max)
    weights = jnp.exp2(scores - new[:, :1]).astype(BF16)
    mixed = jnp.dot(
        weights, jnp.concatenate([values, ones], axis=1), preferred_element_type=F32
    )
    if fresh:
        l_ref[rows, :] = mixed[:, HD:]
        a_ref[rows, :] = mixed[:, :HD]
    else:
        factor = jnp.exp2(old - new)
        l_ref[rows, :] = l_ref[rows, :] * factor + mixed[:, HD:]
        a_ref[rows, :] = a_ref[rows, :] * factor + mixed[:, :HD]
    m_ref[rows, :] = new


def score(asked, keys):
    return lax.dot_general(asked, keys, CONTRACT_LAST, preferred_element_type=F32) * SCALE


def list_visible(place, visible, shifts, chosen):
    my_span = place[0] * NY + place[1]
    count = jnp.int32(0)
    for block, shift in enumerate(shifts):
        first = lax.rem(place[0] + NX - shift, NX) * NY
        for y in range(NY):
            earlier = first + y
            usable = (earlier < my_span) & (visible[my_span, earlier] > 0)

            @pl.when(usable)
            def _():
                chosen[count] = block * NY + y

            count = count + usable.astype(jnp.int32)
    return count


def absorb_prior(count, chosen, q_ref, mine, other, state):
    def block(spans):
        keys = jnp.concatenate([r[s, :, :HD] for s in spans for r in (mine, other)], axis=0)
        values = jnp.concatenate([r[s, :, HD:] for s in spans for r in (mine, other)], axis=0)
        for piece in range(ROWS // HEAD_ROWS):
            rows = slice(piece * HEAD_ROWS, (piece + 1) * HEAD_ROWS)
            tile, h = divmod(piece, GROUP)
            asked = q_ref[tile, h * HEAD_ROWS : (h + 1) * HEAD_ROWS, :]
            absorb(state, rows, score(asked, keys), values, False)

    done = jnp.int32(0)
    for size in (4, 2, 1):

        def step(i, _, size=size, done=done):
            block([chosen[done + size * i + j] for j in range(size)])
            return 0

        turns = (count - done) // size
        lax.fori_loop(0, turns, step, 0)
        done = done + turns * size


def attend_raw(
    place, visible, bpos, q_ref, kv_o, kv_c, kv_z, kv_zc, mine, other, m_ref, l_ref, a_ref, chosen
):
    state = (m_ref, l_ref, a_ref)
    y, z, core = place[1], place[2], place[3]
    g, parity = z // 2, lax.rem(z, 2)
    pieces = (kv_o, kv_c, kv_z, kv_zc)
    here = parity * 256 + core * 128
    lane = lax.broadcasted_iota(jnp.int32, (1, 512), 1)
    combo = lane // 128
    key_at = ((parity ^ (combo // 2)) * 2 + (core ^ (combo % 2))) * 128 + lane % 128
    blane = lax.broadcasted_iota(jnp.int32, (1, 256), 1)
    brow = blane % 128
    beacon_at = (brow // BEA) * 32 + (core ^ (blane // 128)) * BEA + brow % BEA
    raw_rows = lax.broadcasted_iota(jnp.int32, (TOK, 1), 0) + here
    own_keys = jnp.concatenate([mine[y, :, :HD], other[y, :, :HD]], axis=0)
    own_values = jnp.concatenate([mine[y, :, HD:], other[y, :, HD:]], axis=0)

    def tile_step(tile, _):
        source = lax.rem(g - tile + KVH, KVH)
        first = source * 64 + parity * 32 + core * BEA
        at = bpos[pl.ds(pl.multiple_of(first, BEA), BEA), :1] - source * 512
        row_at = jnp.concatenate([raw_rows, at], axis=0)
        rank = first + lax.broadcasted_iota(jnp.int32, (BEA, 1), 0)
        row_rank = jnp.concatenate([jnp.full((TOK, 1), -1, jnp.int32), rank], axis=0)
        keys = jnp.concatenate([r[tile, :TOK, :] for r in pieces] + [own_keys], axis=0)
        values = jnp.concatenate([r[tile, TOK:, :] for r in pieces] + [own_values], axis=0)
        allowed = jnp.concatenate([key_at <= row_at, beacon_at <= row_rank], axis=1)
        base = tile * TILE

        def rows_of(h):
            return pl.ds(pl.multiple_of(base + h * HEAD_ROWS, HEAD_ROWS), HEAD_ROWS)

        for h in range(GROUP):
            asked = q_ref[tile, h * HEAD_ROWS : (h + 1) * HEAD_ROWS, :]
            scores = jnp.where(allowed, score(asked, keys), LOWEST)
            absorb(state, rows_of(h), scores, values, True)

        def earlier_step(e, _):
            there = lax.rem(g - e + KVH, KVH)
            keys = jnp.concatenate([r[there, :TOK, :] for r in pieces], axis=0)
            values = jnp.concatenate([r[there, TOK:, :] for r in pieces], axis=0)
            for h in range(GROUP):
                asked = q_ref[tile, h * HEAD_ROWS : (h + 1) * HEAD_ROWS, :]
                absorb(state, rows_of(h), score(asked, keys), values, False)
            return 0

        lax.fori_loop(0, source, earlier_step, 0)
        return 0

    lax.fori_loop(0, TILES, tile_step, 0)
    count = list_visible(place, visible, (0,), chosen)
    absorb_prior(count, chosen, q_ref, mine, other, state)


def attend_prior(
    shifts, place, visible, q_ref, mine, other, m_in, l_in, a_in, m_ref, l_ref, a_ref, chosen
):
    m_ref[...] = m_in[...]
    l_ref[...] = l_in[...]
    a_ref[...] = a_in[...]
    count = list_visible(place, visible, shifts, chosen)
    absorb_prior(count, chosen, q_ref, mine, other, (m_ref, l_ref, a_ref))


def attend_last(shifts, place, visible, q_ref, mine, other, m_in, l_in, a_in, *rest):
    outs, (m_ref, l_ref, a_ref, chosen) = rest[:TILES], rest[TILES:]
    attend_prior(
        shifts, place, visible, q_ref, mine, other, m_in, l_in, a_in, m_ref, l_ref, a_ref, chosen
    )
    for tile in range(TILES):
        rows = slice(tile * TILE, (tile + 1) * TILE)
        outs[tile][...] = (a_ref[rows, :] / l_ref[rows, :]).astype(BF16)


def unpack_outputs(place, r0, r1, r2, r3, tok_ref, bea_ref):
    g = place[2] // 2
    for step, ref in enumerate((r0, r1, r2, r3)):
        dest = lax.rem(g + step, KVH)
        for h in range(GROUP):
            column = pl.multiple_of((dest * GROUP + h) * HD, HD)
            tok_ref[:, pl.ds(column, HD)] = ref[h * HEAD_ROWS : h * HEAD_ROWS + TOK, :]
            bea_ref[:, pl.ds(column, HD)] = ref[h * HEAD_ROWS + TOK : (h + 1) * HEAD_ROWS, :]


def on_device(q_tok, keys, values, beacon_q, beacon_k, beacon_v, beacon_pos, visible):
    place = jnp.stack([lax.axis_index(a) for a in CHIPS]).astype(jnp.int32)
    to_send = kernel_call(
        pack_beacons,
        "pack_beacons",
        jax.ShapeDtypeStruct((NY * NZ, BEA, 2 * HD), BF16),
        [VMEM] * 2,
        byte_count=600000,
    )(beacon_k, beacon_v)
    arrived = lax.all_to_all(to_send, ("y", "z"), 0, 0, tiled=True)
    block0 = arrived.reshape(NY, HALF, 2 * HD)

    chunks = kernel_call(
        pack_tokens,
        "pack_tokens",
        [jax.ShapeDtypeStruct((TILE + 2 * TOK, HD), BF16)] * TILES,
        [SMEM] + [VMEM] * 4,
        byte_count=1800000,
    )(place, q_tok, keys, values, beacon_q)
    got = [chunks[0]] + [
        lax.ppermute(chunks[step], CHIPS, to_head_group(step)) for step in range(1, TILES)
    ]
    asked = jnp.stack([piece[:TILE] for piece in got])
    kv_o = jnp.stack([piece[TILE:] for piece in got])
    kv_z = lax.ppermute(kv_o, CHIPS, OTHER_PARITY)
    kv_c = lax.ppermute(kv_o, CHIPS, OTHER_CORE)
    kv_zc = lax.ppermute(kv_z, CHIPS, OTHER_CORE)

    from1 = lax.ppermute(block0, CHIPS, to_later_x(1))
    from3 = lax.ppermute(block0, CHIPS, to_later_x(3))
    from2 = lax.ppermute(block0, CHIPS, to_later_x(2))
    block0c = lax.ppermute(block0, CHIPS, OTHER_CORE)
    block13 = jnp.concatenate([from1, from3], axis=0)
    block13c = lax.ppermute(block13, CHIPS, OTHER_CORE)
    block2c = lax.ppermute(from2, CHIPS, OTHER_CORE)

    bpos = jnp.broadcast_to(beacon_pos[:, None], (256, HD))
    state_shape = [jax.ShapeDtypeStruct((ROWS, HD), F32)] * 3
    chosen = pltpu.SMEM((NX * NY,), jnp.int32)
    per_span = ROWS * 256 * HD * 4
    state = kernel_call(
        attend_raw,
        "attend_raw",
        state_shape,
        [SMEM] * 2 + [VMEM] * 8,
        [chosen],
        flops=16 * per_span,
        byte_count=6000000,
    )(place, visible, bpos, asked, kv_o, kv_c, kv_z, kv_zc, block0, block0c)
    state = kernel_call(
        functools.partial(attend_prior, (1, 3)),
        "attend_next",
        state_shape,
        [SMEM] * 2 + [VMEM] * 6,
        [chosen],
        flops=16 * per_span,
        byte_count=9000000,
    )(place, visible, asked, block13, block13c, *state)
    mixed = kernel_call(
        functools.partial(attend_last, (2,)),
        "attend_last",
        [jax.ShapeDtypeStruct((TILE, HD), BF16)] * TILES,
        [SMEM] * 2 + [VMEM] * 6,
        [pltpu.VMEM((ROWS, HD), F32)] * 3 + [chosen],
        flops=8 * per_span,
        byte_count=6000000,
    )(place, visible, asked, from2, block2c, *state)
    back = [mixed[0]] + [
        lax.ppermute(mixed[step], CHIPS, to_head_group(-step)) for step in range(1, TILES)
    ]
    return kernel_call(
        unpack_outputs,
        "unpack_outputs",
        [
            jax.ShapeDtypeStruct((TOK, QH * HD), BF16),
            jax.ShapeDtypeStruct((BEA, QH * HD), BF16),
        ],
        [SMEM] + [VMEM] * 4,
        byte_count=1200000,
    )(place, *back)


def solution(mesh):
    chips = Mesh(mesh.devices.reshape(NX, NY, NZ, NC), CHIPS)
    rows = P(CHIPS, None)
    return jax.shard_map(
        on_device,
        mesh=chips,
        in_specs=(rows, rows, rows, rows, rows, rows, P(("x", "y")), P()),
        out_specs=(rows, rows),
        check_vma=False,
    )
```

```python
import functools

import jax
import jax.numpy as jnp
from jax import lax
from jax.experimental import pallas as pl
from jax.experimental.pallas import tpu as pltpu
from jax.sharding import Mesh, PartitionSpec as P

HD = 128
KVH = 4
QH = 16
GROUP = QH // KVH
NX, NY, NZ, NC = 4, 8, 8, 2
TOK = 128
BEA = 16
HEAD_ROWS = TOK + BEA
TILE = GROUP * HEAD_ROWS
TILES = 4
ROWS = TILES * TILE
HALF = 128
SCALE = HD**-0.5 * 1.4426950408889634
LOWEST = -1e30
CHIPS = ("x", "y", "z", "core")
CONTRACT_LAST = (((1,), (1,)), ((), ()))
VMEM = pl.BlockSpec(memory_space=pltpu.VMEM)
SMEM = pl.BlockSpec(memory_space=pltpu.SMEM)
BF16 = jnp.bfloat16
F32 = jnp.float32


def moves(target):
    pairs = []
    for x in range(NX):
        for y in range(NY):
            for z in range(NZ):
                for core in range(NC):
                    to = target(x, y, z, core)
                    if to is not None:
                        tx, ty, tz, tc = to
                        source = ((x * NY + y) * NZ + z) * NC + core
                        pairs.append((source, ((tx * NY + ty) * NZ + tz % NZ) * NC + tc))
    return pairs


def to_head_group(step):
    return moves(lambda x, y, z, core: (x, y, z + 2 * step, core))


def to_later_x(step):
    return moves(lambda x, y, z, core: (x + step, y, z, core) if x + step < NX else None)


OTHER_CORE = moves(lambda x, y, z, core: (x, y, z, 1 - core))
OTHER_PARITY = moves(lambda x, y, z, core: (x, y, z ^ 1, core))


def kernel_call(body, name, out_shape, in_specs, scratch=(), flops=0, byte_count=0, grid=()):
    return pl.pallas_call(
        body,
        grid=grid,
        name=name,
        out_shape=out_shape,
        in_specs=in_specs,
        out_specs=jax.tree.map(lambda _: VMEM, out_shape),
        scratch_shapes=list(scratch),
        compiler_params=pltpu.CompilerParams(vmem_limit_bytes=20 * 2**20),
        cost_estimate=pl.CostEstimate(
            flops=flops, bytes_accessed=byte_count, transcendentals=0
        ),
    )


def pack_beacons(k_ref, v_ref, out_ref):
    for z in range(NZ):
        g = z // 2
        piece = jnp.concatenate(
            [k_ref[:, g * HD : (g + 1) * HD], v_ref[:, g * HD : (g + 1) * HD]], axis=1
        )
        for y in range(NY):
            out_ref[y * NZ + z] = piece


def pack_tokens(place, q_ref, k_ref, v_ref, bq_ref, *outs):
    g = place[2] // 2
    for step in range(TILES):
        dest = lax.rem(g + step, KVH)
        out = outs[step]
        for h in range(GROUP):
            column = pl.multiple_of((dest * GROUP + h) * HD, HD)
            out[h * HEAD_ROWS : h * HEAD_ROWS + TOK, :] = q_ref[:, pl.ds(column, HD)]
            out[h * HEAD_ROWS + TOK : (h + 1) * HEAD_ROWS, :] = bq_ref[:, pl.ds(column, HD)]
        column = pl.multiple_of(dest * HD, HD)
        out[TILE : TILE + TOK, :] = k_ref[:, pl.ds(column, HD)]
        out[TILE + TOK : TILE + 2 * TOK, :] = v_ref[:, pl.ds(column, HD)]


def absorb(state, rows, scores, values):
    m_ref, l_ref, a_ref = state
    if values.shape[1] == HD:
        values = jnp.concatenate([values, jnp.ones_like(values)], axis=1)
    old = m_ref[rows, :]
    new = jnp.maximum(old, jnp.max(scores, axis=1, keepdims=True))
    weights = jnp.exp2(scores - new[:, :1]).astype(BF16)
    mixed = jnp.dot(weights, values, preferred_element_type=F32)
    factor = jnp.exp2(old - new)
    m_ref[rows, :] = new
    l_ref[rows, :] = l_ref[rows, :] * factor + mixed[:, HD:]
    a_ref[rows, :] = a_ref[rows, :] * factor + mixed[:, :HD]


def score(asked, keys):
    return lax.dot_general(asked, keys, CONTRACT_LAST, preferred_element_type=F32) * SCALE


def list_visible(place, visible, shifts, chosen):
    my_span = place[0] * NY + place[1]
    count = jnp.int32(0)
    for block, shift in enumerate(shifts):
        first = lax.rem(place[0] + NX - shift, NX) * NY
        for y in range(NY):
            earlier = first + y
            usable = (earlier < my_span) & (visible[my_span, earlier] > 0)

            @pl.when(usable)
            def _():
                chosen[count] = block * NY + y

            count = count + usable.astype(jnp.int32)
    return count


def absorb_prior(count, chosen, halves, tiles, sources, k_buf, v_buf):
    v_buf[:, HD:] = jnp.ones((v_buf.shape[0], HD), BF16)

    def block(first, size):
        for j in range(size):
            entry = chosen[first + j]
            rows = slice(j * 2 * HALF, (j + 1) * 2 * HALF)
            for index, refs in enumerate(sources):

                @pl.when(entry // NY == index)
                def _(refs=refs, rows=rows, entry=entry):
                    span = lax.rem(entry, NY)
                    k_buf[rows, :] = jnp.concatenate([r[span, :, :HD] for r in refs], axis=0)
                    v_buf[rows, :HD] = jnp.concatenate([r[span, :, HD:] for r in refs], axis=0)

        keys, values = k_buf[: size * 2 * HALF, :], v_buf[: size * 2 * HALF, :]

        def tile_step(tile, _):
            parts = halves(tile)
            both = [score(asked[...], keys) for asked, _, _ in parts]
            for (_, state, rows), scores in zip(parts, both):
                absorb(state, rows, scores, values)
            return 0

        if tiles == 1:
            tile_step(0, 0)
        else:
            lax.fori_loop(0, tiles, tile_step, 0)

    def full_block(i, _):
        block(4 * i, 4)
        return 0

    full = jnp.maximum(count // 4 - 1, 0)
    lax.fori_loop(0, full, full_block, 0)
    left = count - 4 * full
    for size in range(1, 8):

        @pl.when(left == size)
        def _(size=size):
            block(4 * full, size)


HALVES = (slice(0, TILE // 2), slice(TILE // 2, TILE))


def attend_raw(
    place, bpos, q_ref, kv_o, kv_c, kv_z, kv_zc, mine, other, m_in, l_in, a_in, m_ref, l_ref, a_ref
):
    y, z, core = place[1], place[2], place[3]
    g, parity = z // 2, lax.rem(z, 2)
    pieces = (kv_o, kv_c, kv_z, kv_zc)
    here = parity * 256 + core * 128
    lane = lax.broadcasted_iota(jnp.int32, (1, 512), 1)
    combo = lane // 128
    key_at = ((parity ^ (combo // 2)) * 2 + (core ^ (combo % 2))) * 128 + lane % 128
    blane = lax.broadcasted_iota(jnp.int32, (1, 256), 1)
    brow = blane % 128
    beacon_at = (brow // BEA) * 32 + (core ^ (blane // 128)) * BEA + brow % BEA
    raw_rows = lax.broadcasted_iota(jnp.int32, (TOK, 1), 0) + here
    no_rank = jnp.full((TOK, 1), -1, jnp.int32)
    own_keys = jnp.concatenate([mine[y, :, :HD], other[y, :, :HD]], axis=0)
    own_values = jnp.concatenate([mine[y, :, HD:], other[y, :, HD:]], axis=0)

    m_ref[...] = m_in[...]
    l_ref[...] = l_in[...]
    a_ref[...] = a_in[...]

    def halves(tile):
        state = (m_ref.at[tile], l_ref.at[tile], a_ref.at[tile])
        return [(q_ref.at[tile, rows, :], state, rows) for rows in HALVES]

    def tile_step(tile, _):
        source = lax.rem(g - tile + KVH, KVH)
        first = source * 64 + parity * 32 + core * BEA
        at = bpos[pl.ds(pl.multiple_of(first, BEA), BEA), :1] - source * 512
        row_at = jnp.concatenate([raw_rows, at] * 2, axis=0)
        rank = first + lax.broadcasted_iota(jnp.int32, (BEA, 1), 0)
        row_rank = jnp.concatenate([no_rank, rank] * 2, axis=0)
        keys = jnp.concatenate([r[tile, :TOK, :] for r in pieces] + [own_keys], axis=0)
        values = jnp.concatenate([r[tile, TOK:, :] for r in pieces] + [own_values], axis=0)
        allowed = jnp.concatenate([key_at <= row_at, beacon_at <= row_rank], axis=1)
        parts = halves(tile)
        both = [score(asked[...], keys) for asked, _, _ in parts]
        for (_, state, rows), scores in zip(parts, both):
            absorb(state, rows, jnp.where(allowed, scores, LOWEST), values)

        def earlier_step(e, _):
            there = lax.rem(g - e + KVH, KVH)
            keys = jnp.concatenate([r[there, :TOK, :] for r in pieces], axis=0)
            values = jnp.concatenate([r[there, TOK:, :] for r in pieces], axis=0)
            both = [score(asked[...], keys) for asked, _, _ in parts]
            for (_, state, rows), scores in zip(parts, both):
                absorb(state, rows, scores, values)
            return 0

        lax.fori_loop(0, source, earlier_step, 0)
        return 0

    lax.fori_loop(0, TILES, tile_step, 0)


def attend_own_x(place, visible, q_ref, mine, other, m_ref, l_ref, a_ref, chosen, k_buf, v_buf):
    m_ref[...] = jnp.full(m_ref.shape, LOWEST, F32)
    l_ref[...] = jnp.zeros(l_ref.shape, F32)
    a_ref[...] = jnp.zeros(a_ref.shape, F32)

    def halves(tile):
        state = (m_ref.at[tile], l_ref.at[tile], a_ref.at[tile])
        return [(q_ref.at[tile, rows, :], state, rows) for rows in HALVES]

    count = list_visible(place, visible, (0,), chosen)
    absorb_prior(count, chosen, halves, TILES, ((mine, other),), k_buf, v_buf)


def attend_prior(place, visible, q_ref, *rest):
    sources = tuple((rest[i], rest[3 + i]) for i in range(3))
    m_in, l_in, a_in, out, m_ref, l_ref, a_ref, chosen, k_buf, v_buf = rest[6:]
    m_ref[...] = m_in[0]
    l_ref[...] = l_in[0]
    a_ref[...] = a_in[0]
    state = (m_ref, l_ref, a_ref)
    count = list_visible(place, visible, (1, 3, 2), chosen)

    def halves(_):
        return [(q_ref.at[0, rows, :], state, rows) for rows in HALVES]

    absorb_prior(count, chosen, halves, 1, sources, k_buf, v_buf)
    out[...] = (a_ref[...] / l_ref[...]).astype(BF16)


def unpack_outputs(place, r0, r1, r2, r3, tok_ref, bea_ref):
    g = place[2] // 2
    for step, ref in enumerate((r0, r1, r2, r3)):
        dest = lax.rem(g + step, KVH)
        for h in range(GROUP):
            column = pl.multiple_of((dest * GROUP + h) * HD, HD)
            tok_ref[:, pl.ds(column, HD)] = ref[h * HEAD_ROWS : h * HEAD_ROWS + TOK, :]
            bea_ref[:, pl.ds(column, HD)] = ref[h * HEAD_ROWS + TOK : (h + 1) * HEAD_ROWS, :]


def on_device(q_tok, keys, values, beacon_q, beacon_k, beacon_v, beacon_pos, visible):
    place = jnp.stack([lax.axis_index(a) for a in CHIPS]).astype(jnp.int32)
    bpos = jnp.broadcast_to(beacon_pos[:, None], (256, HD))
    to_send = kernel_call(
        pack_beacons,
        "pack_beacons",
        jax.ShapeDtypeStruct((NY * NZ, BEA, 2 * HD), BF16),
        [VMEM] * 2,
        byte_count=1000,
    )(beacon_k, beacon_v)
    arrived = lax.all_to_all(to_send, ("y", "z"), 0, 0, tiled=True)
    block0 = arrived.reshape(NY, HALF, 2 * HD)

    chunks = kernel_call(
        pack_tokens,
        "pack_tokens",
        [jax.ShapeDtypeStruct((TILE + 2 * TOK, HD), BF16)] * TILES,
        [SMEM] + [VMEM] * 4,
        byte_count=1000,
    )(place, q_tok, keys, values, beacon_q)
    got = [chunks[0]] + [
        lax.ppermute(chunks[step], CHIPS, to_head_group(step)) for step in range(1, TILES)
    ]
    *got, _ = lax.optimization_barrier((*got, block0))
    asked = jnp.stack([piece[:TILE] for piece in got])
    kv_o = jnp.stack([piece[TILE:] for piece in got])
    block0c = lax.ppermute(block0, CHIPS, OTHER_CORE)

    state_shape = [jax.ShapeDtypeStruct((TILES, TILE, HD), F32)] * 3
    chosen = pltpu.SMEM((NX * NY,), jnp.int32)
    buffers = [pltpu.VMEM((7 * 2 * HALF, HD), BF16), pltpu.VMEM((7 * 2 * HALF, 2 * HD), BF16)]
    state = kernel_call(
        attend_own_x,
        "attend_own_x",
        state_shape,
        [SMEM] * 2 + [VMEM] * 3,
        [chosen, *buffers],
        flops=1000,
        byte_count=1000,
    )(place, visible, asked, block0, block0c)
    kv_z = lax.ppermute(kv_o, CHIPS, OTHER_PARITY)
    kv_c = lax.ppermute(kv_o, CHIPS, OTHER_CORE)
    kv_z, _ = lax.optimization_barrier((kv_z, state[1]))
    kv_zc = lax.ppermute(kv_z, CHIPS, OTHER_CORE)
    arriving = [lax.ppermute(block0, CHIPS, to_later_x(step)) for step in (1, 3, 2)]
    *arriving, _ = lax.optimization_barrier((*arriving, kv_zc))
    crossed = [lax.ppermute(block, CHIPS, OTHER_CORE) for block in arriving]
    state = kernel_call(
        attend_raw,
        "attend_raw",
        state_shape,
        [SMEM] + [VMEM] * 11,
        flops=1000,
        byte_count=1000,
    )(place, bpos, asked, kv_o, kv_c, kv_z, kv_zc, block0, block0c, *state)
    mixed = [None] * TILES
    for tile in (2, 1, 3, 0):
        one = pl.BlockSpec((1, TILE, HD), lambda i, tile=tile: (tile, 0, 0))
        mixed[tile] = kernel_call(
            attend_prior,
            f"attend_prior_{tile}",
            jax.ShapeDtypeStruct((TILE, HD), BF16),
            [SMEM] * 2 + [one] + [VMEM] * 6 + [one] * 3,
            [pltpu.VMEM((TILE, HD), F32)] * 3 + [chosen, *buffers],
            grid=(1,),
            flops=1000,
            byte_count=1000,
        )(place, visible, asked, *arriving, *crossed, *state)
    back = [mixed[0]] + [
        lax.ppermute(mixed[step], CHIPS, to_head_group(-step)) for step in range(1, TILES)
    ]
    return kernel_call(
        unpack_outputs,
        "unpack_outputs",
        [
            jax.ShapeDtypeStruct((TOK, QH * HD), BF16),
            jax.ShapeDtypeStruct((BEA, QH * HD), BF16),
        ],
        [SMEM] + [VMEM] * 4,
        byte_count=1000,
    )(place, *back)


def solution(mesh):
    chips = Mesh(mesh.devices.reshape(NX, NY, NZ, NC), CHIPS)
    rows = P(CHIPS, None)
    return jax.shard_map(
        on_device,
        mesh=chips,
        in_specs=(rows, rows, rows, rows, rows, rows, P(("x", "y")), P()),
        out_specs=(rows, rows),
        check_vma=False,
    )
```

```python
import functools

import jax
import jax.numpy as jnp
from jax import lax
from jax.experimental import pallas as pl
from jax.experimental.pallas import tpu as pltpu
from jax.sharding import Mesh, PartitionSpec as P

HD = 128
KVH = 4
QH = 16
GROUP = QH // KVH
NX, NY, NZ, NC = 4, 8, 8, 2
TOK = 128
BEA = 16
HEAD_ROWS = TOK + BEA
TILE = GROUP * HEAD_ROWS
TILES = 4
ROWS = TILES * TILE
HALF = 128
SCALE = HD**-0.5 * 1.4426950408889634
LOWEST = -1e30
CHIPS = ("x", "y", "z", "core")
CONTRACT_LAST = (((1,), (1,)), ((), ()))
VMEM = pl.BlockSpec(memory_space=pltpu.VMEM)
SMEM = pl.BlockSpec(memory_space=pltpu.SMEM)
BF16 = jnp.bfloat16
F32 = jnp.float32


def moves(target):
    pairs = []
    for x in range(NX):
        for y in range(NY):
            for z in range(NZ):
                for core in range(NC):
                    to = target(x, y, z, core)
                    if to is not None:
                        tx, ty, tz, tc = to
                        source = ((x * NY + y) * NZ + z) * NC + core
                        pairs.append((source, ((tx * NY + ty) * NZ + tz % NZ) * NC + tc))
    return pairs


def to_head_group(step):
    return moves(lambda x, y, z, core: (x, y, z + 2 * step, core))


def to_later_x(step):
    return moves(lambda x, y, z, core: (x + step, y, z, core) if x + step < NX else None)


OTHER_CORE = moves(lambda x, y, z, core: (x, y, z, 1 - core))
OTHER_PARITY = moves(lambda x, y, z, core: (x, y, z ^ 1, core))


def kernel_call(body, name, out_shape, in_specs, scratch=(), flops=0, byte_count=0):
    return pl.pallas_call(
        body,
        name=name,
        out_shape=out_shape,
        in_specs=in_specs,
        out_specs=jax.tree.map(lambda _: VMEM, out_shape),
        scratch_shapes=list(scratch),
        compiler_params=pltpu.CompilerParams(vmem_limit_bytes=20 * 2**20),
        cost_estimate=pl.CostEstimate(
            flops=flops, bytes_accessed=byte_count, transcendentals=0
        ),
    )


def pack_beacons(k_ref, v_ref, out_ref):
    for z in range(NZ):
        g = z // 2
        piece = jnp.concatenate(
            [k_ref[:, g * HD : (g + 1) * HD], v_ref[:, g * HD : (g + 1) * HD]], axis=1
        )
        for y in range(NY):
            out_ref[y * NZ + z] = piece


def pack_tokens(place, q_ref, k_ref, v_ref, bq_ref, *outs):
    g = place[2] // 2
    for step in range(TILES):
        dest = lax.rem(g + step, KVH)
        out = outs[step]
        for h in range(GROUP):
            column = pl.multiple_of((dest * GROUP + h) * HD, HD)
            out[h * HEAD_ROWS : h * HEAD_ROWS + TOK, :] = q_ref[:, pl.ds(column, HD)]
            out[h * HEAD_ROWS + TOK : (h + 1) * HEAD_ROWS, :] = bq_ref[:, pl.ds(column, HD)]
        column = pl.multiple_of(dest * HD, HD)
        out[TILE : TILE + TOK, :] = k_ref[:, pl.ds(column, HD)]
        out[TILE + TOK : TILE + 2 * TOK, :] = v_ref[:, pl.ds(column, HD)]


def absorb(state, rows, scores, values):
    m_ref, l_ref, a_ref = state
    old = m_ref[rows, :]
    new = jnp.maximum(old, jnp.max(scores, axis=1, keepdims=True))
    weights = jnp.exp2(scores - new[:, :1]).astype(BF16)
    mixed = jnp.dot(weights, values, preferred_element_type=F32)
    factor = jnp.exp2(old - new)
    m_ref[rows, :] = new
    l_ref[rows, :] = l_ref[rows, :] * factor + mixed[:, HD:]
    a_ref[rows, :] = a_ref[rows, :] * factor + mixed[:, :HD]


def score(asked, keys):
    return lax.dot_general(asked, keys, CONTRACT_LAST, preferred_element_type=F32) * SCALE


def list_visible(place, visible, shifts, chosen):
    my_span = place[0] * NY + place[1]
    count = jnp.int32(0)
    for block, shift in enumerate(shifts):
        first = lax.rem(place[0] + NX - shift, NX) * NY
        for y in range(NY):
            earlier = first + y
            usable = (earlier < my_span) & (visible[my_span, earlier] > 0)

            @pl.when(usable)
            def _():
                chosen[count] = block * NY + y

            count = count + usable.astype(jnp.int32)
    return count


def absorb_prior(count, chosen, halves, tiles, sources, k_buf, v_buf):
    v_buf[:, HD:] = jnp.ones((v_buf.shape[0], HD), BF16)

    def block(first, size):
        for j in range(size):
            entry = chosen[first + j]
            rows = slice(j * 2 * HALF, (j + 1) * 2 * HALF)
            for index, refs in enumerate(sources):

                @pl.when(entry // NY == index)
                def _(refs=refs, rows=rows, entry=entry):
                    span = lax.rem(entry, NY)
                    k_buf[rows, :] = jnp.concatenate([r[span, :, :HD] for r in refs], axis=0)
                    v_buf[rows, :HD] = jnp.concatenate([r[span, :, HD:] for r in refs], axis=0)

        keys, values = k_buf[: size * 2 * HALF, :], v_buf[: size * 2 * HALF, :]

        def tile_step(tile, _):
            parts = halves(tile)
            both = [score(asked[...], keys) for asked, _, _ in parts]
            for (_, state, rows), scores in zip(parts, both):
                absorb(state, rows, scores, values)
            return 0

        if tiles == 1:
            tile_step(0, 0)
        else:
            lax.fori_loop(0, tiles, tile_step, 0)

    def full_block(i, _):
        block(4 * i, 4)
        return 0

    full = jnp.maximum(count // 4 - 1, 0)
    lax.fori_loop(0, full, full_block, 0)
    left = count - 4 * full
    for size in range(1, 8):

        @pl.when(left == size)
        def _(size=size):
            block(4 * full, size)


HALVES = (slice(0, TILE // 2), slice(TILE // 2, TILE))


def attend_raw(
    place, bpos, q_ref, kv_o, kv_c, kv_z, kv_zc, mine, other, m_in, l_in, a_in, m_ref, l_ref, a_ref
):
    y, z, core = place[1], place[2], place[3]
    g, parity = z // 2, lax.rem(z, 2)
    pieces = (kv_o, kv_c, kv_z, kv_zc)
    here = parity * 256 + core * 128
    lane = lax.broadcasted_iota(jnp.int32, (1, 512), 1)
    combo = lane // 128
    key_at = ((parity ^ (combo // 2)) * 2 + (core ^ (combo % 2))) * 128 + lane % 128
    blane = lax.broadcasted_iota(jnp.int32, (1, 256), 1)
    brow = blane % 128
    beacon_at = (brow // BEA) * 32 + (core ^ (blane // 128)) * BEA + brow % BEA
    raw_rows = lax.broadcasted_iota(jnp.int32, (TOK, 1), 0) + here
    no_rank = jnp.full((TOK, 1), -1, jnp.int32)
    own_keys = jnp.concatenate([mine[y, :, :HD], other[y, :, :HD]], axis=0)
    own_values = jnp.concatenate([mine[y, :, HD:], other[y, :, HD:]], axis=0)

    def span_tile(source):
        return lax.rem(g - source + KVH, KVH)

    def ask(source, rows):
        tile = span_tile(source)
        kept = [r[tile, :TOK, :] for r in pieces] + [own_keys]
        kept += [r[span_tile(e), :TOK, :] for e in range(source) for r in pieces]
        return score(q_ref[tile, rows, :], jnp.concatenate(kept, axis=0))

    parts = [(source, rows) for source in (3, 2, 1, 0) for rows in HALVES]
    coming = ask(*parts[0])
    for index, (source, rows) in enumerate(parts):
        scores = coming
        if index + 1 < len(parts):
            coming = ask(*parts[index + 1])
        tile = span_tile(source)
        first = source * 64 + parity * 32 + core * BEA
        at = bpos[pl.ds(pl.multiple_of(first, BEA), BEA), :1] - source * 512
        row_at = jnp.concatenate([raw_rows, at] * 2, axis=0)
        rank = first + lax.broadcasted_iota(jnp.int32, (BEA, 1), 0)
        row_rank = jnp.concatenate([no_rank, rank] * 2, axis=0)
        allowed = jnp.concatenate([key_at <= row_at, beacon_at <= row_rank], axis=1)
        near = jnp.where(allowed, scores[:, :768], LOWEST)
        scores = jnp.concatenate([near, scores[:, 768:]], axis=1) if source else near
        kept = [r[tile, TOK:, :] for r in pieces] + [own_values]
        kept += [r[span_tile(e), TOK:, :] for e in range(source) for r in pieces]
        values = jnp.concatenate(kept, axis=0)
        old = m_in[tile, rows, :]
        new = jnp.maximum(old, jnp.max(scores, axis=1, keepdims=True))
        weights = jnp.exp2(scores - new[:, :1]).astype(BF16)
        mixed = jnp.dot(
            weights,
            jnp.concatenate([values, jnp.ones_like(values)], axis=1),
            preferred_element_type=F32,
        )
        factor = jnp.exp2(old - new)
        m_ref[tile, rows, :] = new
        l_ref[tile, rows, :] = l_in[tile, rows, :] * factor + mixed[:, HD:]
        a_ref[tile, rows, :] = a_in[tile, rows, :] * factor + mixed[:, :HD]


def attend_own_x(place, visible, q_ref, mine, other, m_ref, l_ref, a_ref, chosen, k_buf, v_buf):
    m_ref[...] = jnp.full(m_ref.shape, LOWEST, F32)
    l_ref[...] = jnp.zeros(l_ref.shape, F32)
    a_ref[...] = jnp.zeros(a_ref.shape, F32)

    def halves(tile):
        state = (m_ref.at[tile], l_ref.at[tile], a_ref.at[tile])
        return [(q_ref.at[tile, rows, :], state, rows) for rows in HALVES]

    count = list_visible(place, visible, (0,), chosen)
    absorb_prior(count, chosen, halves, TILES, ((mine, other),), k_buf, v_buf)


def attend_prior(tile, place, visible, q_ref, *rest):
    sources = tuple((rest[i], rest[3 + i]) for i in range(3))
    m_in, l_in, a_in, out, m_ref, l_ref, a_ref, chosen, k_buf, v_buf = rest[6:]
    m_ref[...] = m_in[tile]
    l_ref[...] = l_in[tile]
    a_ref[...] = a_in[tile]
    state = (m_ref, l_ref, a_ref)
    count = list_visible(place, visible, (1, 3, 2), chosen)

    def halves(_):
        return [(q_ref.at[tile, rows, :], state, rows) for rows in HALVES]

    absorb_prior(count, chosen, halves, 1, sources, k_buf, v_buf)
    out[...] = (a_ref[...] / l_ref[...]).astype(BF16)


def unpack_outputs(place, r0, r1, r2, r3, tok_ref, bea_ref):
    g = place[2] // 2
    for step, ref in enumerate((r0, r1, r2, r3)):
        dest = lax.rem(g + step, KVH)
        for h in range(GROUP):
            column = pl.multiple_of((dest * GROUP + h) * HD, HD)
            tok_ref[:, pl.ds(column, HD)] = ref[h * HEAD_ROWS : h * HEAD_ROWS + TOK, :]
            bea_ref[:, pl.ds(column, HD)] = ref[h * HEAD_ROWS + TOK : (h + 1) * HEAD_ROWS, :]


def on_device(q_tok, keys, values, beacon_q, beacon_k, beacon_v, beacon_pos, visible):
    place = jnp.stack([lax.axis_index(a) for a in CHIPS]).astype(jnp.int32)
    bpos = jnp.broadcast_to(beacon_pos[:, None], (256, HD))
    to_send = kernel_call(
        pack_beacons,
        "pack_beacons",
        jax.ShapeDtypeStruct((NY * NZ, BEA, 2 * HD), BF16),
        [VMEM] * 2,
        byte_count=1000,
    )(beacon_k, beacon_v)
    arrived = lax.all_to_all(to_send, ("y", "z"), 0, 0, tiled=True)
    block0 = arrived.reshape(NY, HALF, 2 * HD)

    chunks = kernel_call(
        pack_tokens,
        "pack_tokens",
        [jax.ShapeDtypeStruct((TILE + 2 * TOK, HD), BF16)] * TILES,
        [SMEM] + [VMEM] * 4,
        byte_count=1000,
    )(place, q_tok, keys, values, beacon_q)
    got = [chunks[0]] + [
        lax.ppermute(chunks[step], CHIPS, to_head_group(step)) for step in range(1, TILES)
    ]
    *got, _ = lax.optimization_barrier((*got, block0))
    asked = jnp.stack([piece[:TILE] for piece in got])
    kv_o = jnp.stack([piece[TILE:] for piece in got])
    block0c = lax.ppermute(block0, CHIPS, OTHER_CORE)

    state_shape = [jax.ShapeDtypeStruct((TILES, TILE, HD), F32)] * 3
    chosen = pltpu.SMEM((NX * NY,), jnp.int32)
    buffers = [pltpu.VMEM((7 * 2 * HALF, HD), BF16), pltpu.VMEM((7 * 2 * HALF, 2 * HD), BF16)]
    state = kernel_call(
        attend_own_x,
        "attend_own_x",
        state_shape,
        [SMEM] * 2 + [VMEM] * 3,
        [chosen, *buffers],
        flops=1000,
        byte_count=1000,
    )(place, visible, asked, block0, block0c)
    kv_z = lax.ppermute(kv_o, CHIPS, OTHER_PARITY)
    kv_c = lax.ppermute(kv_o, CHIPS, OTHER_CORE)
    kv_z, _ = lax.optimization_barrier((kv_z, state[1]))
    kv_zc = lax.ppermute(kv_z, CHIPS, OTHER_CORE)
    state = kernel_call(
        attend_raw,
        "attend_raw",
        state_shape,
        [SMEM] + [VMEM] * 11,
        flops=1000,
        byte_count=1000,
    )(place, bpos, asked, kv_o, kv_c, kv_z, kv_zc, block0, block0c, *state)
    arriving = [lax.ppermute(block0, CHIPS, to_later_x(step)) for step in (1, 3, 2)]
    *arriving, _ = lax.optimization_barrier((*arriving, state[1]))
    crossed = [lax.ppermute(block, CHIPS, OTHER_CORE) for block in arriving]
    mixed = [None] * TILES
    for tile in (2, 1, 3, 0):
        mixed[tile] = kernel_call(
            functools.partial(attend_prior, tile),
            f"attend_prior_{tile}",
            jax.ShapeDtypeStruct((TILE, HD), BF16),
            [SMEM] * 2 + [VMEM] * 10,
            [pltpu.VMEM((TILE, HD), F32)] * 3 + [chosen, *buffers],
            flops=1000,
            byte_count=1000,
        )(place, visible, asked, *arriving, *crossed, *state)
    back = [mixed[0]] + [
        lax.ppermute(mixed[step], CHIPS, to_head_group(-step)) for step in range(1, TILES)
    ]
    return kernel_call(
        unpack_outputs,
        "unpack_outputs",
        [
            jax.ShapeDtypeStruct((TOK, QH * HD), BF16),
            jax.ShapeDtypeStruct((BEA, QH * HD), BF16),
        ],
        [SMEM] + [VMEM] * 4,
        byte_count=1000,
    )(place, *back)


def solution(mesh):
    chips = Mesh(mesh.devices.reshape(NX, NY, NZ, NC), CHIPS)
    rows = P(CHIPS, None)
    return jax.shard_map(
        on_device,
        mesh=chips,
        in_specs=(rows, rows, rows, rows, rows, rows, P(("x", "y")), P()),
        out_specs=(rows, rows),
        check_vma=False,
    )
```

```python
import functools

import jax
import jax.numpy as jnp
from jax import lax
from jax.experimental import pallas as pl
from jax.experimental.pallas import tpu as pltpu
from jax.sharding import Mesh, PartitionSpec as P

HD = 128
KVH = 4
QH = 16
GROUP = QH // KVH
NX, NY, NZ, NC = 4, 8, 8, 2
TOK = 128
BEA = 16
HEAD_ROWS = TOK + BEA
TILE = GROUP * HEAD_ROWS
TILES = 4
ROWS = TILES * TILE
HALF = 128
SCALE = HD**-0.5 * 1.4426950408889634
LOWEST = -1e30
CHIPS = ("x", "y", "z", "core")
CONTRACT_LAST = (((1,), (1,)), ((), ()))
VMEM = pl.BlockSpec(memory_space=pltpu.VMEM)
SMEM = pl.BlockSpec(memory_space=pltpu.SMEM)
BF16 = jnp.bfloat16
F32 = jnp.float32


def moves(target):
    pairs = []
    for x in range(NX):
        for y in range(NY):
            for z in range(NZ):
                for core in range(NC):
                    to = target(x, y, z, core)
                    if to is not None:
                        tx, ty, tz, tc = to
                        source = ((x * NY + y) * NZ + z) * NC + core
                        pairs.append((source, ((tx * NY + ty) * NZ + tz % NZ) * NC + tc))
    return pairs


def to_head_group(step):
    return moves(lambda x, y, z, core: (x, y, z + 2 * step, core))


def to_later_x(step):
    return moves(lambda x, y, z, core: (x + step, y, z, core) if x + step < NX else None)


OTHER_CORE = moves(lambda x, y, z, core: (x, y, z, 1 - core))
OTHER_PARITY = moves(lambda x, y, z, core: (x, y, z ^ 1, core))


def kernel_call(body, name, out_shape, in_specs, scratch=(), flops=0, byte_count=0):
    return pl.pallas_call(
        body,
        name=name,
        out_shape=out_shape,
        in_specs=in_specs,
        out_specs=jax.tree.map(lambda _: VMEM, out_shape),
        scratch_shapes=list(scratch),
        compiler_params=pltpu.CompilerParams(vmem_limit_bytes=20 * 2**20),
        cost_estimate=pl.CostEstimate(
            flops=flops, bytes_accessed=byte_count, transcendentals=0
        ),
    )


def pack_beacons(k_ref, v_ref, out_ref):
    for z in range(NZ):
        g = z // 2
        piece = jnp.concatenate(
            [k_ref[:, g * HD : (g + 1) * HD], v_ref[:, g * HD : (g + 1) * HD]], axis=1
        )
        for y in range(NY):
            out_ref[y * NZ + z] = piece


def pack_tokens(place, q_ref, k_ref, v_ref, bq_ref, *outs):
    g = place[2] // 2
    for step in range(TILES):
        dest = lax.rem(g + step, KVH)
        out = outs[step]
        for h in range(GROUP):
            column = pl.multiple_of((dest * GROUP + h) * HD, HD)
            out[h * HEAD_ROWS : h * HEAD_ROWS + TOK, :] = q_ref[:, pl.ds(column, HD)]
            out[h * HEAD_ROWS + TOK : (h + 1) * HEAD_ROWS, :] = bq_ref[:, pl.ds(column, HD)]
        column = pl.multiple_of(dest * HD, HD)
        out[TILE : TILE + TOK, :] = k_ref[:, pl.ds(column, HD)]
        out[TILE + TOK : TILE + 2 * TOK, :] = v_ref[:, pl.ds(column, HD)]


def absorb(state, rows, scores, values):
    m_ref, l_ref, a_ref = state
    old = m_ref[rows, :]
    new = jnp.maximum(old, jnp.max(scores, axis=1, keepdims=True))
    weights = jnp.exp2(scores - new[:, :1]).astype(BF16)
    mixed = jnp.dot(weights, values, preferred_element_type=F32)
    factor = jnp.exp2(old - new)
    m_ref[rows, :] = new
    l_ref[rows, :] = l_ref[rows, :] * factor + mixed[:, HD:]
    a_ref[rows, :] = a_ref[rows, :] * factor + mixed[:, :HD]


def score(asked, keys):
    return lax.dot_general(asked, keys, CONTRACT_LAST, preferred_element_type=F32) * SCALE


def list_visible(place, visible, shifts, chosen):
    my_span = place[0] * NY + place[1]
    count = jnp.int32(0)
    for block, shift in enumerate(shifts):
        first = lax.rem(place[0] + NX - shift, NX) * NY
        for y in range(NY):
            earlier = first + y
            usable = (earlier < my_span) & (visible[my_span, earlier] > 0)

            @pl.when(usable)
            def _():
                chosen[count] = block * NY + y

            count = count + usable.astype(jnp.int32)
    return count


def absorb_parts(asked, state_of, parts, keys, values):
    coming = score(asked(*parts[0]), keys)
    for index, part in enumerate(parts):
        scores = coming
        if index + 1 < len(parts):
            coming = score(asked(*parts[index + 1]), keys)
        absorb(state_of(part[0]), part[1], scores, values)


def absorb_block(first, size, count, chosen, sources, k_buf, v_buf, run):
    for j in range(size):
        rows = slice(j * 2 * HALF, (j + 1) * 2 * HALF)
        entry = chosen[jnp.minimum(first + j, count - 1)]
        real = first + j < count
        for index, refs in enumerate(sources):

            @pl.when(entry // NY == index)
            def _(refs=refs, rows=rows, entry=entry, real=real):
                span = lax.rem(entry, NY)
                k_buf[rows, :] = jnp.concatenate([r[span, :, :HD] for r in refs], axis=0)

                @pl.when(real)
                def _():
                    v_buf[rows, :HD] = jnp.concatenate([r[span, :, HD:] for r in refs], axis=0)
                    v_buf[rows, HD:] = jnp.ones((2 * HALF, HD), BF16)

                @pl.when(jnp.logical_not(real))
                def _():
                    v_buf[rows, :] = jnp.zeros((2 * HALF, 2 * HD), BF16)

    run(k_buf[: size * 2 * HALF, :], v_buf[: size * 2 * HALF, :])


def absorb_few(count, chosen, sources, k_buf, v_buf, run):
    for size in (4, 6, 8):

        @pl.when((count > (0 if size == 4 else size - 2)) & (count <= size))
        def _(size=size):
            absorb_block(0, size, count, chosen, sources, k_buf, v_buf, run)


def absorb_many(count, chosen, sources, k_buf, v_buf, run):
    left = lax.rem(count, 4)
    fold = (left > 0) & (left < 3) & (count > 4)
    blocks = jnp.where(fold, count // 4 - 1, (count + 3) // 4)

    def step(i, _):
        absorb_block(4 * i, 4, count, chosen, sources, k_buf, v_buf, run)
        return 0

    lax.fori_loop(0, blocks, step, 0)

    @pl.when(fold)
    def _():
        absorb_block(4 * blocks, 6, count, chosen, sources, k_buf, v_buf, run)


HALVES = (slice(0, TILE // 2), slice(TILE // 2, TILE))
PARTS = [(tile, rows) for tile in range(TILES) for rows in HALVES]


def over_tiles(q_ref, m_ref, l_ref, a_ref):
    def asked(tile, rows):
        return q_ref[tile, rows, :]

    def state_of(tile):
        return (m_ref.at[tile], l_ref.at[tile], a_ref.at[tile])

    return asked, state_of


def attend_raw(
    place, visible, bpos, q_ref, kv_o, kv_c, kv_z, kv_zc, mine, other, *rest
):
    m_ref, l_ref, a_ref, chosen, k_buf, v_buf = rest
    y, z, core = place[1], place[2], place[3]
    g, parity = z // 2, lax.rem(z, 2)
    pieces = (kv_o, kv_c, kv_z, kv_zc)
    here = parity * 256 + core * 128
    lane = lax.broadcasted_iota(jnp.int32, (1, 512), 1)
    combo = lane // 128
    key_at = ((parity ^ (combo // 2)) * 2 + (core ^ (combo % 2))) * 128 + lane % 128
    blane = lax.broadcasted_iota(jnp.int32, (1, 256), 1)
    brow = blane % 128
    beacon_at = (brow // BEA) * 32 + (core ^ (blane // 128)) * BEA + brow % BEA
    raw_rows = lax.broadcasted_iota(jnp.int32, (TOK, 1), 0) + here
    no_rank = jnp.full((TOK, 1), -1, jnp.int32)
    own_keys = jnp.concatenate([mine[y, :, :HD], other[y, :, :HD]], axis=0)
    own_values = jnp.concatenate([mine[y, :, HD:], other[y, :, HD:]], axis=0)

    def span_tile(source):
        return lax.rem(g - source + KVH, KVH)

    def ask(source, rows):
        tile = span_tile(source)
        kept = [r[tile, :TOK, :] for r in pieces] + [own_keys]
        kept += [r[span_tile(e), :TOK, :] for e in range(source) for r in pieces]
        return score(q_ref[tile, rows, :], jnp.concatenate(kept, axis=0))

    parts = [(source, rows) for source in (3, 2, 1, 0) for rows in HALVES]
    coming = ask(*parts[0])
    for index, (source, rows) in enumerate(parts):
        scores = coming
        if index + 1 < len(parts):
            coming = ask(*parts[index + 1])
        tile = span_tile(source)
        first = source * 64 + parity * 32 + core * BEA
        at = bpos[pl.ds(pl.multiple_of(first, BEA), BEA), :1] - source * 512
        row_at = jnp.concatenate([raw_rows, at] * 2, axis=0)
        rank = first + lax.broadcasted_iota(jnp.int32, (BEA, 1), 0)
        row_rank = jnp.concatenate([no_rank, rank] * 2, axis=0)
        allowed = jnp.concatenate([key_at <= row_at, beacon_at <= row_rank], axis=1)
        near = jnp.where(allowed, scores[:, :768], LOWEST)
        scores = jnp.concatenate([near, scores[:, 768:]], axis=1) if source else near
        kept = [r[tile, TOK:, :] for r in pieces] + [own_values]
        kept += [r[span_tile(e), TOK:, :] for e in range(source) for r in pieces]
        values = jnp.concatenate(kept, axis=0)
        new = jnp.max(scores, axis=1, keepdims=True)
        weights = jnp.exp2(scores - new).astype(BF16)
        mixed = jnp.dot(
            weights,
            jnp.concatenate([values, jnp.ones_like(values)], axis=1),
            preferred_element_type=F32,
        )
        m_ref[tile, rows, :] = jnp.broadcast_to(new, (TILE // 2, HD))
        l_ref[tile, rows, :] = mixed[:, HD:]
        a_ref[tile, rows, :] = mixed[:, :HD]

    count = list_visible(place, visible, (0,), chosen)
    absorb_few(
        count,
        chosen,
        ((mine, other),),
        k_buf,
        v_buf,
        functools.partial(absorb_parts, *over_tiles(q_ref, m_ref, l_ref, a_ref), PARTS),
    )


def attend_next(place, visible, q_ref, mine1, mine3, other1, other3, m_in, l_in, a_in, *rest):
    m_ref, l_ref, a_ref, chosen, k_buf, v_buf = rest
    m_ref[...] = m_in[...]
    l_ref[...] = l_in[...]
    a_ref[...] = a_in[...]
    count = list_visible(place, visible, (1, 3), chosen)
    absorb_many(
        count,
        chosen,
        ((mine1, other1), (mine3, other3)),
        k_buf,
        v_buf,
        functools.partial(absorb_parts, *over_tiles(q_ref, m_ref, l_ref, a_ref), PARTS),
    )


def attend_last(tile, place, visible, q_ref, mine, other, m_in, l_in, a_in, out, *rest):
    m_ref, l_ref, a_ref, chosen, k_buf, v_buf = rest
    m_ref[...] = m_in[tile]
    l_ref[...] = l_in[tile]
    a_ref[...] = a_in[tile]
    count = list_visible(place, visible, (2,), chosen)

    def asked(_, rows):
        return q_ref[tile, rows, :]

    def state_of(_):
        return (m_ref, l_ref, a_ref)

    run = functools.partial(absorb_parts, asked, state_of, PARTS[:2])
    absorb_few(count, chosen, ((mine, other),), k_buf, v_buf, run)
    out[...] = (a_ref[...] / l_ref[...]).astype(BF16)


def unpack_outputs(place, r0, r1, r2, r3, tok_ref, bea_ref):
    g = place[2] // 2
    for step, ref in enumerate((r0, r1, r2, r3)):
        dest = lax.rem(g + step, KVH)
        for h in range(GROUP):
            column = pl.multiple_of((dest * GROUP + h) * HD, HD)
            tok_ref[:, pl.ds(column, HD)] = ref[h * HEAD_ROWS : h * HEAD_ROWS + TOK, :]
            bea_ref[:, pl.ds(column, HD)] = ref[h * HEAD_ROWS + TOK : (h + 1) * HEAD_ROWS, :]


def on_device(q_tok, keys, values, beacon_q, beacon_k, beacon_v, beacon_pos, visible):
    place = jnp.stack([lax.axis_index(a) for a in CHIPS]).astype(jnp.int32)
    bpos = jnp.broadcast_to(beacon_pos[:, None], (256, HD))
    chunks = kernel_call(
        pack_tokens,
        "pack_tokens",
        [jax.ShapeDtypeStruct((TILE + 2 * TOK, HD), BF16)] * TILES,
        [SMEM] + [VMEM] * 4,
        byte_count=1000,
    )(place, q_tok, keys, values, beacon_q)
    got = [chunks[0]] + [
        lax.ppermute(chunks[step], CHIPS, to_head_group(step)) for step in range(1, TILES)
    ]
    to_send = kernel_call(
        pack_beacons,
        "pack_beacons",
        jax.ShapeDtypeStruct((NY * NZ, BEA, 2 * HD), BF16),
        [VMEM] * 2,
        byte_count=1000,
    )(beacon_k, beacon_v)
    to_send, _ = lax.optimization_barrier((to_send, got[1]))
    arrived = lax.all_to_all(to_send, ("y", "z"), 0, 0, tiled=True)
    block0 = arrived.reshape(NY, HALF, 2 * HD)

    asked = jnp.stack([piece[:TILE] for piece in got])
    kv_o = jnp.stack([piece[TILE:] for piece in got])
    kv_z = lax.ppermute(kv_o, CHIPS, OTHER_PARITY)
    kv_c = lax.ppermute(kv_o, CHIPS, OTHER_CORE)
    kv_zc = lax.ppermute(kv_z, CHIPS, OTHER_CORE)
    block0c = lax.ppermute(block0, CHIPS, OTHER_CORE)
    arriving = [lax.ppermute(block0, CHIPS, to_later_x(step)) for step in (1, 3, 2)]

    state_shape = [jax.ShapeDtypeStruct((TILES, TILE, HD), F32)] * 3
    scratch = [
        pltpu.SMEM((NX * NY,), jnp.int32),
        pltpu.VMEM((NY * 2 * HALF, HD), BF16),
        pltpu.VMEM((NY * 2 * HALF, 2 * HD), BF16),
    ]
    state = kernel_call(
        attend_raw,
        "attend_raw",
        state_shape,
        [SMEM] * 2 + [VMEM] * 8,
        scratch,
        flops=1000,
        byte_count=1000,
    )(place, visible, bpos, asked, kv_o, kv_c, kv_z, kv_zc, block0, block0c)
    near = list(lax.optimization_barrier((*arriving[:2], state[1]))[:2])
    near_crossed = [lax.ppermute(block, CHIPS, OTHER_CORE) for block in near]
    state = kernel_call(
        attend_next,
        "attend_next",
        state_shape,
        [SMEM] * 2 + [VMEM] * 8,
        scratch,
        flops=1000,
        byte_count=1000,
    )(place, visible, asked, *near, *near_crossed, *state)
    far = arriving[2]
    far_crossed = lax.ppermute(far, CHIPS, OTHER_CORE)
    mixed = [None] * TILES
    for tile in (2, 1, 3, 0):
        mixed[tile] = kernel_call(
            functools.partial(attend_last, tile),
            f"attend_last_{tile}",
            jax.ShapeDtypeStruct((TILE, HD), BF16),
            [SMEM] * 2 + [VMEM] * 6,
            [pltpu.VMEM((TILE, HD), F32)] * 3 + scratch,
            flops=1000,
            byte_count=1000,
        )(place, visible, asked, far, far_crossed, *state)
    back = [mixed[0]] + [
        lax.ppermute(mixed[step], CHIPS, to_head_group(-step)) for step in range(1, TILES)
    ]
    return kernel_call(
        unpack_outputs,
        "unpack_outputs",
        [
            jax.ShapeDtypeStruct((TOK, QH * HD), BF16),
            jax.ShapeDtypeStruct((BEA, QH * HD), BF16),
        ],
        [SMEM] + [VMEM] * 4,
        byte_count=1000,
    )(place, *back)


def solution(mesh):
    chips = Mesh(mesh.devices.reshape(NX, NY, NZ, NC), CHIPS)
    rows = P(CHIPS, None)
    return jax.shard_map(
        on_device,
        mesh=chips,
        in_specs=(rows, rows, rows, rows, rows, rows, P(("x", "y")), P()),
        out_specs=(rows, rows),
        check_vma=False,
    )
```

```python
import functools

import jax
import jax.numpy as jnp
from jax import lax
from jax.experimental import pallas as pl
from jax.experimental.pallas import tpu as pltpu
from jax.sharding import Mesh, PartitionSpec as P

HD = 128
KVH = 4
QH = 16
GROUP = QH // KVH
NX, NY, NZ, NC = 4, 8, 8, 2
TOK = 128
BEA = 16
HEAD_ROWS = TOK + BEA
TILE = GROUP * HEAD_ROWS
TILES = 4
ROWS = TILES * TILE
HALF = 128
SCALE = HD**-0.5 * 1.4426950408889634
LOWEST = -1e30
CHIPS = ("x", "y", "z", "core")
CONTRACT_LAST = (((1,), (1,)), ((), ()))
VMEM = pl.BlockSpec(memory_space=pltpu.VMEM)
SMEM = pl.BlockSpec(memory_space=pltpu.SMEM)
BF16 = jnp.bfloat16
F32 = jnp.float32


def moves(target):
    pairs = []
    for x in range(NX):
        for y in range(NY):
            for z in range(NZ):
                for core in range(NC):
                    to = target(x, y, z, core)
                    if to is not None:
                        tx, ty, tz, tc = to
                        source = ((x * NY + y) * NZ + z) * NC + core
                        pairs.append((source, ((tx * NY + ty) * NZ + tz % NZ) * NC + tc))
    return pairs


def to_head_group(step):
    return moves(lambda x, y, z, core: (x, y, z + 2 * step, core))


def to_later_x(step):
    return moves(lambda x, y, z, core: (x + step, y, z, core) if x + step < NX else None)


OTHER_CORE = moves(lambda x, y, z, core: (x, y, z, 1 - core))
OTHER_PARITY = moves(lambda x, y, z, core: (x, y, z ^ 1, core))


def kernel_call(body, name, out_shape, in_specs, scratch=(), flops=0, byte_count=0):
    return pl.pallas_call(
        body,
        name=name,
        out_shape=out_shape,
        in_specs=in_specs,
        out_specs=jax.tree.map(lambda _: VMEM, out_shape),
        scratch_shapes=list(scratch),
        compiler_params=pltpu.CompilerParams(vmem_limit_bytes=20 * 2**20),
        cost_estimate=pl.CostEstimate(
            flops=flops, bytes_accessed=byte_count, transcendentals=0
        ),
    )


def pack_beacons(k_ref, v_ref, out_ref):
    for z in range(NZ):
        g = z // 2
        piece = jnp.concatenate(
            [k_ref[:, g * HD : (g + 1) * HD], v_ref[:, g * HD : (g + 1) * HD]], axis=1
        )
        for y in range(NY):
            out_ref[y * NZ + z] = piece


def pack_tokens(place, q_ref, k_ref, v_ref, bq_ref, *outs):
    g = place[2] // 2
    for step in range(TILES):
        dest = lax.rem(g + step, KVH)
        out = outs[step]
        for h in range(GROUP):
            column = pl.multiple_of((dest * GROUP + h) * HD, HD)
            out[h * HEAD_ROWS : h * HEAD_ROWS + TOK, :] = q_ref[:, pl.ds(column, HD)]
            out[h * HEAD_ROWS + TOK : (h + 1) * HEAD_ROWS, :] = bq_ref[:, pl.ds(column, HD)]
        column = pl.multiple_of(dest * HD, HD)
        out[TILE : TILE + TOK, :] = k_ref[:, pl.ds(column, HD)]
        out[TILE + TOK : TILE + 2 * TOK, :] = v_ref[:, pl.ds(column, HD)]


def absorb(state, rows, scores, values):
    m_ref, l_ref, a_ref = state
    old = m_ref[rows, :]
    new = jnp.maximum(old, jnp.max(scores, axis=1, keepdims=True))
    weights = jnp.exp2(scores - new[:, :1]).astype(BF16)
    mixed = jnp.dot(weights, values, preferred_element_type=F32)
    factor = jnp.exp2(old - new)
    m_ref[rows, :] = new
    l_ref[rows, :] = l_ref[rows, :] * factor + mixed[:, HD:]
    a_ref[rows, :] = a_ref[rows, :] * factor + mixed[:, :HD]


def score(asked, keys):
    return lax.dot_general(asked, keys, CONTRACT_LAST, preferred_element_type=F32) * SCALE


def list_visible(place, visible, shifts, chosen):
    my_span = place[0] * NY + place[1]
    count = jnp.int32(0)
    for block, shift in enumerate(shifts):
        first = lax.rem(place[0] + NX - shift, NX) * NY
        for y in range(NY):
            earlier = first + y
            usable = (earlier < my_span) & (visible[my_span, earlier] > 0)

            @pl.when(usable)
            def _():
                chosen[count] = block * NY + y

            count = count + usable.astype(jnp.int32)
    return count


def absorb_tile(asked, state, keys, values):
    both = [score(asked[rows, :], keys) for rows in HALVES]
    for rows, scores in zip(HALVES, both):
        absorb(state, rows, scores, values)


def absorb_block(first, size, count, chosen, sources, k_buf, v_buf, run):
    for j in range(size):
        rows = slice(j * 2 * HALF, (j + 1) * 2 * HALF)
        entry = chosen[jnp.minimum(first + j, count - 1)]
        real = first + j < count
        for index, refs in enumerate(sources):

            @pl.when(entry // NY == index)
            def _(refs=refs, rows=rows, entry=entry, real=real):
                span = lax.rem(entry, NY)
                k_buf[rows, :] = jnp.concatenate([r[span, :, :HD] for r in refs], axis=0)

                @pl.when(real)
                def _():
                    v_buf[rows, :HD] = jnp.concatenate([r[span, :, HD:] for r in refs], axis=0)
                    v_buf[rows, HD:] = jnp.ones((2 * HALF, HD), BF16)

                @pl.when(jnp.logical_not(real))
                def _():
                    v_buf[rows, :] = jnp.zeros((2 * HALF, 2 * HD), BF16)

    run(k_buf[: size * 2 * HALF, :], v_buf[: size * 2 * HALF, :])


def absorb_many(count, chosen, sources, k_buf, v_buf, run):
    left = lax.rem(count, 4)
    fold = (left > 0) & (left < 3) & (count > 4)
    blocks = jnp.where(fold, count // 4 - 1, (count + 3) // 4)

    def step(i, _):
        absorb_block(4 * i, 4, count, chosen, sources, k_buf, v_buf, run)
        return 0

    lax.fori_loop(0, blocks, step, 0)

    @pl.when(fold)
    def _():
        absorb_block(4 * blocks, 6, count, chosen, sources, k_buf, v_buf, run)


HALVES = (slice(0, TILE // 2), slice(TILE // 2, TILE))


def over_tiles(q_ref, m_ref, l_ref, a_ref, keys, values):
    def tile_step(tile, _):
        state = (m_ref.at[tile], l_ref.at[tile], a_ref.at[tile])
        absorb_tile(q_ref.at[tile], state, keys, values)
        return 0

    lax.fori_loop(0, TILES, tile_step, 0)


def attend_raw(
    place, bpos, q_ref, kv_o, kv_c, kv_z, kv_zc, mine, other, m_in, l_in, a_in, m_ref, l_ref, a_ref
):
    y, z, core = place[1], place[2], place[3]
    g, parity = z // 2, lax.rem(z, 2)
    pieces = (kv_o, kv_c, kv_z, kv_zc)
    here = parity * 256 + core * 128
    lane = lax.broadcasted_iota(jnp.int32, (1, 512), 1)
    combo = lane // 128
    key_at = ((parity ^ (combo // 2)) * 2 + (core ^ (combo % 2))) * 128 + lane % 128
    blane = lax.broadcasted_iota(jnp.int32, (1, 256), 1)
    brow = blane % 128
    beacon_at = (brow // BEA) * 32 + (core ^ (blane // 128)) * BEA + brow % BEA
    raw_rows = lax.broadcasted_iota(jnp.int32, (TOK, 1), 0) + here
    no_rank = jnp.full((TOK, 1), -1, jnp.int32)
    own_keys = jnp.concatenate([mine[y, :, :HD], other[y, :, :HD]], axis=0)
    own_values = jnp.concatenate([mine[y, :, HD:], other[y, :, HD:]], axis=0)

    def span_tile(source):
        return lax.rem(g - source + KVH, KVH)

    def ask(source, rows):
        tile = span_tile(source)
        kept = [r[tile, :TOK, :] for r in pieces] + [own_keys]
        kept += [r[span_tile(e), :TOK, :] for e in range(source) for r in pieces]
        return score(q_ref[tile, rows, :], jnp.concatenate(kept, axis=0))

    parts = [(source, rows) for source in (3, 2, 1, 0) for rows in HALVES]
    coming = ask(*parts[0])
    for index, (source, rows) in enumerate(parts):
        scores = coming
        if index + 1 < len(parts):
            coming = ask(*parts[index + 1])
        tile = span_tile(source)
        first = source * 64 + parity * 32 + core * BEA
        at = bpos[pl.ds(pl.multiple_of(first, BEA), BEA), :1] - source * 512
        row_at = jnp.concatenate([raw_rows, at] * 2, axis=0)
        rank = first + lax.broadcasted_iota(jnp.int32, (BEA, 1), 0)
        row_rank = jnp.concatenate([no_rank, rank] * 2, axis=0)
        allowed = jnp.concatenate([key_at <= row_at, beacon_at <= row_rank], axis=1)
        near = jnp.where(allowed, scores[:, :768], LOWEST)
        scores = jnp.concatenate([near, scores[:, 768:]], axis=1) if source else near
        kept = [r[tile, TOK:, :] for r in pieces] + [own_values]
        kept += [r[span_tile(e), TOK:, :] for e in range(source) for r in pieces]
        values = jnp.concatenate(kept, axis=0)
        old = m_in[tile, rows, :]
        new = jnp.maximum(old, jnp.max(scores, axis=1, keepdims=True))
        weights = jnp.exp2(scores - new[:, :1]).astype(BF16)
        mixed = jnp.dot(
            weights,
            jnp.concatenate([values, jnp.ones_like(values)], axis=1),
            preferred_element_type=F32,
        )
        factor = jnp.exp2(old - new)
        m_ref[tile, rows, :] = new
        l_ref[tile, rows, :] = l_in[tile, rows, :] * factor + mixed[:, HD:]
        a_ref[tile, rows, :] = a_in[tile, rows, :] * factor + mixed[:, :HD]


def attend_own_x(place, visible, q_ref, mine, other, m_ref, l_ref, a_ref, chosen, k_buf, v_buf):
    m_ref[...] = jnp.full(m_ref.shape, LOWEST, F32)
    l_ref[...] = jnp.zeros(l_ref.shape, F32)
    a_ref[...] = jnp.zeros(a_ref.shape, F32)
    count = list_visible(place, visible, (0,), chosen)
    run = functools.partial(over_tiles, q_ref, m_ref, l_ref, a_ref)
    absorb_many(count, chosen, ((mine, other),), k_buf, v_buf, run)


def attend_next(place, visible, q_ref, mine1, mine3, other1, other3, m_in, l_in, a_in, *rest):
    m_ref, l_ref, a_ref, chosen, k_buf, v_buf = rest
    m_ref[...] = m_in[...]
    l_ref[...] = l_in[...]
    a_ref[...] = a_in[...]
    count = list_visible(place, visible, (1, 3), chosen)
    absorb_many(
        count,
        chosen,
        ((mine1, other1), (mine3, other3)),
        k_buf,
        v_buf,
        functools.partial(over_tiles, q_ref, m_ref, l_ref, a_ref),
    )


def attend_last(tile, place, visible, q_ref, mine, other, m_in, l_in, a_in, out, *rest):
    m_ref, l_ref, a_ref, chosen, k_buf, v_buf = rest
    m_ref[...] = m_in[tile]
    l_ref[...] = l_in[tile]
    a_ref[...] = a_in[tile]
    count = list_visible(place, visible, (2,), chosen)

    run = functools.partial(absorb_tile, q_ref.at[tile], (m_ref, l_ref, a_ref))
    absorb_many(count, chosen, ((mine, other),), k_buf, v_buf, run)
    out[...] = (a_ref[...] / l_ref[...]).astype(BF16)


def unpack_outputs(place, r0, r1, r2, r3, tok_ref, bea_ref):
    g = place[2] // 2
    for step, ref in enumerate((r0, r1, r2, r3)):
        dest = lax.rem(g + step, KVH)
        for h in range(GROUP):
            column = pl.multiple_of((dest * GROUP + h) * HD, HD)
            tok_ref[:, pl.ds(column, HD)] = ref[h * HEAD_ROWS : h * HEAD_ROWS + TOK, :]
            bea_ref[:, pl.ds(column, HD)] = ref[h * HEAD_ROWS + TOK : (h + 1) * HEAD_ROWS, :]


def on_device(q_tok, keys, values, beacon_q, beacon_k, beacon_v, beacon_pos, visible):
    place = jnp.stack([lax.axis_index(a) for a in CHIPS]).astype(jnp.int32)
    bpos = jnp.broadcast_to(beacon_pos[:, None], (256, HD))
    chunks = kernel_call(
        pack_tokens,
        "pack_tokens",
        [jax.ShapeDtypeStruct((TILE + 2 * TOK, HD), BF16)] * TILES,
        [SMEM] + [VMEM] * 4,
        byte_count=1000,
    )(place, q_tok, keys, values, beacon_q)
    got = [chunks[0]] + [
        lax.ppermute(chunks[step], CHIPS, to_head_group(step)) for step in range(1, TILES)
    ]
    to_send = kernel_call(
        pack_beacons,
        "pack_beacons",
        jax.ShapeDtypeStruct((NY * NZ, BEA, 2 * HD), BF16),
        [VMEM] * 2,
        byte_count=1000,
    )(beacon_k, beacon_v)
    arrived = lax.all_to_all(to_send, ("y", "z"), 0, 0, tiled=True)
    block0 = arrived.reshape(NY, HALF, 2 * HD)

    *got, _ = lax.optimization_barrier((*got, block0))
    asked = jnp.stack([piece[:TILE] for piece in got])
    kv_o = jnp.stack([piece[TILE:] for piece in got])
    block0c = lax.ppermute(block0, CHIPS, OTHER_CORE)

    state_shape = [jax.ShapeDtypeStruct((TILES, TILE, HD), F32)] * 3
    scratch = [
        pltpu.SMEM((NX * NY,), jnp.int32),
        pltpu.VMEM((6 * 2 * HALF, HD), BF16),
        pltpu.VMEM((6 * 2 * HALF, 2 * HD), BF16),
    ]
    state = kernel_call(
        attend_own_x,
        "attend_own_x",
        state_shape,
        [SMEM] * 2 + [VMEM] * 3,
        scratch,
        flops=1000,
        byte_count=1000,
    )(place, visible, asked, block0, block0c)
    kv_z = lax.ppermute(kv_o, CHIPS, OTHER_PARITY)
    kv_c = lax.ppermute(kv_o, CHIPS, OTHER_CORE)
    kv_z, _ = lax.optimization_barrier((kv_z, state[1]))
    kv_zc = lax.ppermute(kv_z, CHIPS, OTHER_CORE)
    state = kernel_call(
        attend_raw,
        "attend_raw",
        state_shape,
        [SMEM] + [VMEM] * 11,
        flops=1000,
        byte_count=1000,
    )(place, bpos, asked, kv_o, kv_c, kv_z, kv_zc, block0, block0c, *state)
    arriving = [lax.ppermute(block0, CHIPS, to_later_x(step)) for step in (1, 3, 2)]
    *near, far, _ = lax.optimization_barrier((*arriving, state[1]))
    near_crossed = [lax.ppermute(block, CHIPS, OTHER_CORE) for block in near]
    state = kernel_call(
        attend_next,
        "attend_next",
        state_shape,
        [SMEM] * 2 + [VMEM] * 8,
        scratch,
        flops=1000,
        byte_count=1000,
    )(place, visible, asked, *near, *near_crossed, *state)
    far_crossed = lax.ppermute(far, CHIPS, OTHER_CORE)
    mixed = [None] * TILES
    for tile in (2, 1, 3, 0):
        mixed[tile] = kernel_call(
            functools.partial(attend_last, tile),
            f"attend_last_{tile}",
            jax.ShapeDtypeStruct((TILE, HD), BF16),
            [SMEM] * 2 + [VMEM] * 6,
            [pltpu.VMEM((TILE, HD), F32)] * 3 + scratch,
            flops=1000,
            byte_count=1000,
        )(place, visible, asked, far, far_crossed, *state)
    back = [mixed[0]] + [
        lax.ppermute(mixed[step], CHIPS, to_head_group(-step)) for step in range(1, TILES)
    ]
    return kernel_call(
        unpack_outputs,
        "unpack_outputs",
        [
            jax.ShapeDtypeStruct((TOK, QH * HD), BF16),
            jax.ShapeDtypeStruct((BEA, QH * HD), BF16),
        ],
        [SMEM] + [VMEM] * 4,
        byte_count=1000,
    )(place, *back)


def solution(mesh):
    chips = Mesh(mesh.devices.reshape(NX, NY, NZ, NC), CHIPS)
    rows = P(CHIPS, None)
    return jax.shard_map(
        on_device,
        mesh=chips,
        in_specs=(rows, rows, rows, rows, rows, rows, P(("x", "y")), P()),
        out_specs=(rows, rows),
        check_vma=False,
    )
```

```python
import functools

import jax
import jax.numpy as jnp
from jax import lax
from jax.experimental import pallas as pl
from jax.experimental.pallas import tpu as pltpu
from jax.sharding import Mesh, PartitionSpec as P

HD = 128
KVH = 4
QH = 16
GROUP = QH // KVH
NX, NY, NZ, NC = 4, 8, 8, 2
TOK = 128
BEA = 16
HEAD_ROWS = TOK + BEA
TILE = GROUP * HEAD_ROWS
TILES = 4
ROWS = TILES * TILE
HALF = 128
SCALE = HD**-0.5 * 1.4426950408889634
LOWEST = -1e30
CHIPS = ("x", "y", "z", "core")
CONTRACT_LAST = (((1,), (1,)), ((), ()))
VMEM = pl.BlockSpec(memory_space=pltpu.VMEM)
SMEM = pl.BlockSpec(memory_space=pltpu.SMEM)
BF16 = jnp.bfloat16
F32 = jnp.float32


def moves(target):
    pairs = []
    for x in range(NX):
        for y in range(NY):
            for z in range(NZ):
                for core in range(NC):
                    to = target(x, y, z, core)
                    if to is not None:
                        tx, ty, tz, tc = to
                        source = ((x * NY + y) * NZ + z) * NC + core
                        pairs.append((source, ((tx * NY + ty) * NZ + tz % NZ) * NC + tc))
    return pairs


def to_head_group(step):
    return moves(lambda x, y, z, core: (x, y, z + 2 * step, core))


def to_later_x(step):
    return moves(lambda x, y, z, core: (x + step, y, z, core) if x + step < NX else None)


OTHER_CORE = moves(lambda x, y, z, core: (x, y, z, 1 - core))
OTHER_PARITY = moves(lambda x, y, z, core: (x, y, z ^ 1, core))


def kernel_call(body, name, out_shape, in_specs, scratch=(), flops=0, byte_count=0):
    return pl.pallas_call(
        body,
        name=name,
        out_shape=out_shape,
        in_specs=in_specs,
        out_specs=jax.tree.map(lambda _: VMEM, out_shape),
        scratch_shapes=list(scratch),
        compiler_params=pltpu.CompilerParams(vmem_limit_bytes=20 * 2**20),
        cost_estimate=pl.CostEstimate(
            flops=flops, bytes_accessed=byte_count, transcendentals=0
        ),
    )


def pack_beacons(k_ref, v_ref, out_ref):
    for z in range(NZ):
        g = z // 2
        piece = jnp.concatenate(
            [k_ref[:, g * HD : (g + 1) * HD], v_ref[:, g * HD : (g + 1) * HD]], axis=1
        )
        for y in range(NY):
            out_ref[y * NZ + z] = piece


def pack_tokens(place, q_ref, k_ref, v_ref, bq_ref, *outs):
    g = place[2] // 2
    for step in range(TILES):
        dest = lax.rem(g + step, KVH)
        out = outs[step]
        for h in range(GROUP):
            column = pl.multiple_of((dest * GROUP + h) * HD, HD)
            out[h * HEAD_ROWS : h * HEAD_ROWS + TOK, :] = q_ref[:, pl.ds(column, HD)]
            out[h * HEAD_ROWS + TOK : (h + 1) * HEAD_ROWS, :] = bq_ref[:, pl.ds(column, HD)]
        column = pl.multiple_of(dest * HD, HD)
        out[TILE : TILE + TOK, :] = k_ref[:, pl.ds(column, HD)]
        out[TILE + TOK : TILE + 2 * TOK, :] = v_ref[:, pl.ds(column, HD)]


def absorb(state, rows, scores, values):
    m_ref, l_ref, a_ref = state
    old = m_ref[rows, :]
    new = jnp.maximum(old, jnp.max(scores, axis=1, keepdims=True))
    weights = jnp.exp2(scores - new[:, :1]).astype(BF16)
    mixed = jnp.dot(weights, values, preferred_element_type=F32)
    factor = jnp.exp2(old - new)
    m_ref[rows, :] = new
    l_ref[rows, :] = l_ref[rows, :] * factor + mixed[:, HD:]
    a_ref[rows, :] = a_ref[rows, :] * factor + mixed[:, :HD]


def score(asked, keys):
    return lax.dot_general(asked, keys, CONTRACT_LAST, preferred_element_type=F32) * SCALE


def list_visible(place, visible, shifts, chosen):
    my_span = place[0] * NY + place[1]
    count = jnp.int32(0)
    for block, shift in enumerate(shifts):
        first = lax.rem(place[0] + NX - shift, NX) * NY
        for y in range(NY):
            earlier = first + y
            usable = (earlier < my_span) & (visible[my_span, earlier] > 0)

            @pl.when(usable)
            def _():
                chosen[count] = block * NY + y

            count = count + usable.astype(jnp.int32)
    return count


def absorb_tile(asked, state, keys, values):
    both = [score(asked[rows, :], keys) for rows in HALVES]
    for rows, scores in zip(HALVES, both):
        absorb(state, rows, scores, values)


def absorb_block(first, size, count, chosen, sources, k_buf, v_buf, run):
    for j in range(size):
        rows = slice(j * 2 * HALF, (j + 1) * 2 * HALF)
        entry = chosen[jnp.minimum(first + j, count - 1)]
        real = first + j < count
        for index, refs in enumerate(sources):

            @pl.when(entry // NY == index)
            def _(refs=refs, rows=rows, entry=entry, real=real):
                span = lax.rem(entry, NY)
                k_buf[rows, :] = jnp.concatenate([r[span, :, :HD] for r in refs], axis=0)

                @pl.when(real)
                def _():
                    v_buf[rows, :HD] = jnp.concatenate([r[span, :, HD:] for r in refs], axis=0)
                    v_buf[rows, HD:] = jnp.ones((2 * HALF, HD), BF16)

                @pl.when(jnp.logical_not(real))
                def _():
                    v_buf[rows, :] = jnp.zeros((2 * HALF, 2 * HD), BF16)

    run(k_buf[: size * 2 * HALF, :], v_buf[: size * 2 * HALF, :])


def absorb_many(count, chosen, sources, k_buf, v_buf, run):
    left = lax.rem(count, 4)
    fold = (left > 0) & (left < 3) & (count > 4)
    blocks = jnp.where(fold, count // 4 - 1, (count + 3) // 4)

    def step(i, _):
        absorb_block(4 * i, 4, count, chosen, sources, k_buf, v_buf, run)
        return 0

    lax.fori_loop(0, blocks, step, 0)

    @pl.when(fold)
    def _():
        absorb_block(4 * blocks, 6, count, chosen, sources, k_buf, v_buf, run)


HALVES = (slice(0, TILE // 2), slice(TILE // 2, TILE))


def over_tiles(q_ref, first, m_ref, l_ref, a_ref, keys, values):
    def tile_step(tile, _):
        state = (m_ref.at[tile], l_ref.at[tile], a_ref.at[tile])
        absorb_tile(q_ref.at[first + tile], state, keys, values)
        return 0

    lax.fori_loop(0, m_ref.shape[0], tile_step, 0)


def attend_raw(
    place, bpos, q_ref, kv_o, kv_c, kv_z, kv_zc, mine, other, m_in, l_in, a_in, m_ref, l_ref, a_ref
):
    y, z, core = place[1], place[2], place[3]
    g, parity = z // 2, lax.rem(z, 2)
    pieces = (kv_o, kv_c, kv_z, kv_zc)
    here = parity * 256 + core * 128
    lane = lax.broadcasted_iota(jnp.int32, (1, 512), 1)
    combo = lane // 128
    key_at = ((parity ^ (combo // 2)) * 2 + (core ^ (combo % 2))) * 128 + lane % 128
    blane = lax.broadcasted_iota(jnp.int32, (1, 256), 1)
    brow = blane % 128
    beacon_at = (brow // BEA) * 32 + (core ^ (blane // 128)) * BEA + brow % BEA
    raw_rows = lax.broadcasted_iota(jnp.int32, (TOK, 1), 0) + here
    no_rank = jnp.full((TOK, 1), -1, jnp.int32)
    own_keys = jnp.concatenate([mine[y, :, :HD], other[y, :, :HD]], axis=0)
    own_values = jnp.concatenate([mine[y, :, HD:], other[y, :, HD:]], axis=0)

    def span_tile(source):
        return lax.rem(g - source + KVH, KVH)

    def ask(source, rows):
        tile = span_tile(source)
        kept = [r[tile, :TOK, :] for r in pieces] + [own_keys]
        kept += [r[span_tile(e), :TOK, :] for e in range(source) for r in pieces]
        return score(q_ref[tile, rows, :], jnp.concatenate(kept, axis=0))

    parts = [(source, rows) for source in (3, 2, 1, 0) for rows in HALVES]
    coming = ask(*parts[0])
    for index, (source, rows) in enumerate(parts):
        scores = coming
        if index + 1 < len(parts):
            coming = ask(*parts[index + 1])
        tile = span_tile(source)
        first = source * 64 + parity * 32 + core * BEA
        at = bpos[pl.ds(pl.multiple_of(first, BEA), BEA), :1] - source * 512
        row_at = jnp.concatenate([raw_rows, at] * 2, axis=0)
        rank = first + lax.broadcasted_iota(jnp.int32, (BEA, 1), 0)
        row_rank = jnp.concatenate([no_rank, rank] * 2, axis=0)
        allowed = jnp.concatenate([key_at <= row_at, beacon_at <= row_rank], axis=1)
        near = jnp.where(allowed, scores[:, :768], LOWEST)
        scores = jnp.concatenate([near, scores[:, 768:]], axis=1) if source else near
        kept = [r[tile, TOK:, :] for r in pieces] + [own_values]
        kept += [r[span_tile(e), TOK:, :] for e in range(source) for r in pieces]
        values = jnp.concatenate(kept, axis=0)
        old = m_in[tile, rows, :]
        new = jnp.maximum(old, jnp.max(scores, axis=1, keepdims=True))
        weights = jnp.exp2(scores - new[:, :1]).astype(BF16)
        mixed = jnp.dot(
            weights,
            jnp.concatenate([values, jnp.ones_like(values)], axis=1),
            preferred_element_type=F32,
        )
        factor = jnp.exp2(old - new)
        m_ref[tile, rows, :] = new
        l_ref[tile, rows, :] = l_in[tile, rows, :] * factor + mixed[:, HD:]
        a_ref[tile, rows, :] = a_in[tile, rows, :] * factor + mixed[:, :HD]


def attend_own_x(place, visible, q_ref, mine, other, m_ref, l_ref, a_ref, chosen, k_buf, v_buf):
    m_ref[...] = jnp.full(m_ref.shape, LOWEST, F32)
    l_ref[...] = jnp.zeros(l_ref.shape, F32)
    a_ref[...] = jnp.zeros(a_ref.shape, F32)
    count = list_visible(place, visible, (0,), chosen)
    run = functools.partial(over_tiles, q_ref, 0, m_ref, l_ref, a_ref)
    absorb_many(count, chosen, ((mine, other),), k_buf, v_buf, run)


def attend_prior(first, place, visible, q_ref, *rest):
    sources = tuple(zip(rest[:3], rest[3:6]))
    m_in, l_in, a_in, *outs = rest[6:-6]
    m_ref, l_ref, a_ref, chosen, k_buf, v_buf = rest[-6:]
    tiles = pl.ds(first, len(outs))
    m_ref[...] = m_in[tiles]
    l_ref[...] = l_in[tiles]
    a_ref[...] = a_in[tiles]
    count = list_visible(place, visible, (1, 3, 2), chosen)
    run = functools.partial(over_tiles, q_ref, first, m_ref, l_ref, a_ref)
    absorb_many(count, chosen, sources, k_buf, v_buf, run)
    for tile, out in enumerate(outs):
        out[...] = (a_ref[tile] / l_ref[tile]).astype(BF16)


def unpack_outputs(place, r0, r1, r2, r3, tok_ref, bea_ref):
    g = place[2] // 2
    for step, ref in enumerate((r0, r1, r2, r3)):
        dest = lax.rem(g + step, KVH)
        for h in range(GROUP):
            column = pl.multiple_of((dest * GROUP + h) * HD, HD)
            tok_ref[:, pl.ds(column, HD)] = ref[h * HEAD_ROWS : h * HEAD_ROWS + TOK, :]
            bea_ref[:, pl.ds(column, HD)] = ref[h * HEAD_ROWS + TOK : (h + 1) * HEAD_ROWS, :]


def on_device(q_tok, keys, values, beacon_q, beacon_k, beacon_v, beacon_pos, visible):
    place = jnp.stack([lax.axis_index(a) for a in CHIPS]).astype(jnp.int32)
    bpos = jnp.broadcast_to(beacon_pos[:, None], (256, HD))
    chunks = kernel_call(
        pack_tokens,
        "pack_tokens",
        [jax.ShapeDtypeStruct((TILE + 2 * TOK, HD), BF16)] * TILES,
        [SMEM] + [VMEM] * 4,
        byte_count=1000,
    )(place, q_tok, keys, values, beacon_q)
    got = [chunks[0]] + [
        lax.ppermute(chunks[step], CHIPS, to_head_group(step)) for step in range(1, TILES)
    ]
    to_send = kernel_call(
        pack_beacons,
        "pack_beacons",
        jax.ShapeDtypeStruct((NY * NZ, BEA, 2 * HD), BF16),
        [VMEM] * 2,
        byte_count=1000,
    )(beacon_k, beacon_v)
    arrived = lax.all_to_all(to_send, ("y", "z"), 0, 0, tiled=True)
    block0 = arrived.reshape(NY, HALF, 2 * HD)

    *got, _ = lax.optimization_barrier((*got, block0))
    asked = jnp.stack([piece[:TILE] for piece in got])
    kv_o = jnp.stack([piece[TILE:] for piece in got])
    block0c = lax.ppermute(block0, CHIPS, OTHER_CORE)

    state_shape = [jax.ShapeDtypeStruct((TILES, TILE, HD), F32)] * 3
    scratch = [
        pltpu.SMEM((NX * NY,), jnp.int32),
        pltpu.VMEM((6 * 2 * HALF, HD), BF16),
        pltpu.VMEM((6 * 2 * HALF, 2 * HD), BF16),
    ]
    state = kernel_call(
        attend_own_x,
        "attend_own_x",
        state_shape,
        [SMEM] * 2 + [VMEM] * 3,
        scratch,
        flops=1000,
        byte_count=1000,
    )(place, visible, asked, block0, block0c)
    kv_z = lax.ppermute(kv_o, CHIPS, OTHER_PARITY)
    kv_c = lax.ppermute(kv_o, CHIPS, OTHER_CORE)
    kv_z, _ = lax.optimization_barrier((kv_z, state[1]))
    kv_zc = lax.ppermute(kv_z, CHIPS, OTHER_CORE)
    state = kernel_call(
        attend_raw,
        "attend_raw",
        state_shape,
        [SMEM] + [VMEM] * 11,
        flops=1000,
        byte_count=1000,
    )(place, bpos, asked, kv_o, kv_c, kv_z, kv_zc, block0, block0c, *state)
    arriving = [lax.ppermute(block0, CHIPS, to_later_x(step)) for step in (1, 3, 2)]
    *arriving, _ = lax.optimization_barrier((*arriving, state[1]))
    crossed = [lax.ppermute(block, CHIPS, OTHER_CORE) for block in arriving]
    mixed = []
    for first, tiles in ((1, 3), (0, 1)):
        mixed = list(
            kernel_call(
                functools.partial(attend_prior, first),
                f"attend_prior_{first}",
                [jax.ShapeDtypeStruct((TILE, HD), BF16)] * tiles,
                [SMEM] * 2 + [VMEM] * 10,
                [pltpu.VMEM((tiles, TILE, HD), F32)] * 3 + scratch,
                flops=1000,
                byte_count=1000,
            )(place, visible, asked, *arriving, *crossed, *state)
        ) + mixed
    back = [mixed[0]] + [
        lax.ppermute(mixed[step], CHIPS, to_head_group(-step)) for step in range(1, TILES)
    ]
    return kernel_call(
        unpack_outputs,
        "unpack_outputs",
        [
            jax.ShapeDtypeStruct((TOK, QH * HD), BF16),
            jax.ShapeDtypeStruct((BEA, QH * HD), BF16),
        ],
        [SMEM] + [VMEM] * 4,
        byte_count=1000,
    )(place, *back)


def solution(mesh):
    chips = Mesh(mesh.devices.reshape(NX, NY, NZ, NC), CHIPS)
    rows = P(CHIPS, None)
    return jax.shard_map(
        on_device,
        mesh=chips,
        in_specs=(rows, rows, rows, rows, rows, rows, P(("x", "y")), P()),
        out_specs=(rows, rows),
        check_vma=False,
    )
```

```python
import functools

import jax
import jax.numpy as jnp
from jax import lax
from jax.experimental import pallas as pl
from jax.experimental.pallas import tpu as pltpu
from jax.sharding import Mesh, PartitionSpec as P

HD = 128
KVH = 4
QH = 16
GROUP = QH // KVH
NX, NY, NZ, NC = 4, 8, 8, 2
TOK = 128
BEA = 16
HEAD_ROWS = TOK + BEA
TILE = GROUP * HEAD_ROWS
TILES = 4
ROWS = TILES * TILE
HALF = 128
SCALE = HD**-0.5 * 1.4426950408889634
LOWEST = -1e30
CHIPS = ("x", "y", "z", "core")
CONTRACT_LAST = (((1,), (1,)), ((), ()))
VMEM = pl.BlockSpec(memory_space=pltpu.VMEM)
SMEM = pl.BlockSpec(memory_space=pltpu.SMEM)
BF16 = jnp.bfloat16
F32 = jnp.float32


def moves(target):
    pairs = []
    for x in range(NX):
        for y in range(NY):
            for z in range(NZ):
                for core in range(NC):
                    to = target(x, y, z, core)
                    if to is not None:
                        tx, ty, tz, tc = to
                        source = ((x * NY + y) * NZ + z) * NC + core
                        pairs.append((source, ((tx * NY + ty) * NZ + tz % NZ) * NC + tc))
    return pairs


def to_head_group(step):
    return moves(lambda x, y, z, core: (x, y, z + 2 * step, core))


def to_later_x(step):
    return moves(lambda x, y, z, core: (x + step, y, z, core) if x + step < NX else None)


OTHER_CORE = moves(lambda x, y, z, core: (x, y, z, 1 - core))
OTHER_PARITY = moves(lambda x, y, z, core: (x, y, z ^ 1, core))


def kernel_call(body, name, out_shape, in_specs, scratch=(), flops=0, byte_count=0):
    return pl.pallas_call(
        body,
        name=name,
        out_shape=out_shape,
        in_specs=in_specs,
        out_specs=jax.tree.map(lambda _: VMEM, out_shape),
        scratch_shapes=list(scratch),
        compiler_params=pltpu.CompilerParams(vmem_limit_bytes=20 * 2**20),
        cost_estimate=pl.CostEstimate(
            flops=flops, bytes_accessed=byte_count, transcendentals=0
        ),
    )


def pack_beacons(k_ref, v_ref, out_ref):
    for z in range(NZ):
        g = z // 2
        piece = jnp.concatenate(
            [k_ref[:, g * HD : (g + 1) * HD], v_ref[:, g * HD : (g + 1) * HD]], axis=1
        )
        for y in range(NY):
            out_ref[y * NZ + z] = piece


def pack_tokens(place, q_ref, k_ref, v_ref, bq_ref, *outs):
    g = place[2] // 2
    for step in range(TILES):
        dest = lax.rem(g + step, KVH)
        out = outs[step]
        for h in range(GROUP):
            column = pl.multiple_of((dest * GROUP + h) * HD, HD)
            out[h * HEAD_ROWS : h * HEAD_ROWS + TOK, :] = q_ref[:, pl.ds(column, HD)]
            out[h * HEAD_ROWS + TOK : (h + 1) * HEAD_ROWS, :] = bq_ref[:, pl.ds(column, HD)]
        column = pl.multiple_of(dest * HD, HD)
        out[TILE : TILE + TOK, :] = k_ref[:, pl.ds(column, HD)]
        out[TILE + TOK : TILE + 2 * TOK, :] = v_ref[:, pl.ds(column, HD)]


def absorb(state, rows, scores, values):
    m_ref, l_ref, a_ref = state
    old = m_ref[rows, :]
    new = jnp.maximum(old, jnp.max(scores, axis=1, keepdims=True))
    weights = jnp.exp2(scores - new[:, :1]).astype(BF16)
    mixed = jnp.dot(weights, values, preferred_element_type=F32)
    factor = jnp.exp2(old - new)
    m_ref[rows, :] = new
    l_ref[rows, :] = l_ref[rows, :] * factor + mixed[:, HD:]
    a_ref[rows, :] = a_ref[rows, :] * factor + mixed[:, :HD]


def score(asked, keys):
    return lax.dot_general(asked, keys, CONTRACT_LAST, preferred_element_type=F32) * SCALE


def list_visible(place, visible, shifts, chosen):
    my_span = place[0] * NY + place[1]
    count = jnp.int32(0)
    for block, shift in enumerate(shifts):
        first = lax.rem(place[0] + NX - shift, NX) * NY
        for y in range(NY):
            earlier = first + y
            usable = (earlier < my_span) & (visible[my_span, earlier] > 0)

            @pl.when(usable)
            def _():
                chosen[count] = block * NY + y

            count = count + usable.astype(jnp.int32)
    return count


def absorb_tile(asked, state, keys, values):
    both = [score(asked[rows, :], keys) for rows in HALVES]
    for rows, scores in zip(HALVES, both):
        absorb(state, rows, scores, values)


def absorb_block(first, size, count, chosen, sources, k_buf, v_buf, run):
    for j in range(size):
        rows = slice(j * 2 * HALF, (j + 1) * 2 * HALF)
        entry = chosen[jnp.minimum(first + j, count - 1)]
        real = first + j < count
        for index, refs in enumerate(sources):

            @pl.when(entry // NY == index)
            def _(refs=refs, rows=rows, entry=entry, real=real):
                span = lax.rem(entry, NY)
                k_buf[rows, :] = jnp.concatenate([r[span, :, :HD] for r in refs], axis=0)

                @pl.when(real)
                def _():
                    v_buf[rows, :HD] = jnp.concatenate([r[span, :, HD:] for r in refs], axis=0)
                    v_buf[rows, HD:] = jnp.ones((2 * HALF, HD), BF16)

                @pl.when(jnp.logical_not(real))
                def _():
                    v_buf[rows, :] = jnp.zeros((2 * HALF, 2 * HD), BF16)

    run(k_buf[: size * 2 * HALF, :], v_buf[: size * 2 * HALF, :])


def absorb_many(count, chosen, sources, k_buf, v_buf, run):
    left = lax.rem(count, 4)
    fold = (left > 0) & (left < 3) & (count > 4)
    blocks = jnp.where(fold, count // 4 - 1, (count + 3) // 4)

    def step(i, _):
        absorb_block(4 * i, 4, count, chosen, sources, k_buf, v_buf, run)
        return 0

    lax.fori_loop(0, blocks, step, 0)

    @pl.when(fold)
    def _():
        absorb_block(4 * blocks, 6, count, chosen, sources, k_buf, v_buf, run)


HALVES = (slice(0, TILE // 2), slice(TILE // 2, TILE))


def over_tiles(q_ref, first, m_ref, l_ref, a_ref, keys, values):
    def tile_step(tile, _):
        state = (m_ref.at[tile], l_ref.at[tile], a_ref.at[tile])
        absorb_tile(q_ref.at[first + tile], state, keys, values)
        return 0

    lax.fori_loop(0, m_ref.shape[0], tile_step, 0)


def attend_raw(
    place, bpos, q_ref, kv_o, kv_c, kv_z, kv_zc, mine, other, m_in, l_in, a_in, m_ref, l_ref, a_ref
):
    y, z, core = place[1], place[2], place[3]
    g, parity = z // 2, lax.rem(z, 2)
    pieces = (kv_o, kv_c, kv_z, kv_zc)
    here = parity * 256 + core * 128
    lane = lax.broadcasted_iota(jnp.int32, (1, 512), 1)
    combo = lane // 128
    key_at = ((parity ^ (combo // 2)) * 2 + (core ^ (combo % 2))) * 128 + lane % 128
    blane = lax.broadcasted_iota(jnp.int32, (1, 256), 1)
    brow = blane % 128
    beacon_at = (brow // BEA) * 32 + (core ^ (blane // 128)) * BEA + brow % BEA
    raw_rows = lax.broadcasted_iota(jnp.int32, (TOK, 1), 0) + here
    no_rank = jnp.full((TOK, 1), -1, jnp.int32)
    own_keys = jnp.concatenate([mine[y, :, :HD], other[y, :, :HD]], axis=0)
    own_values = jnp.concatenate([mine[y, :, HD:], other[y, :, HD:]], axis=0)

    def span_tile(source):
        return lax.rem(g - source + KVH, KVH)

    def ask(source, rows):
        tile = span_tile(source)
        kept = [r[tile, :TOK, :] for r in pieces] + [own_keys]
        kept += [r[span_tile(e), :TOK, :] for e in range(source) for r in pieces]
        return score(q_ref[tile, rows, :], jnp.concatenate(kept, axis=0))

    parts = [(source, rows) for source in (3, 2, 1, 0) for rows in HALVES]
    coming = ask(*parts[0])
    for index, (source, rows) in enumerate(parts):
        scores = coming
        if index + 1 < len(parts):
            coming = ask(*parts[index + 1])
        tile = span_tile(source)
        first = source * 64 + parity * 32 + core * BEA
        at = bpos[pl.ds(pl.multiple_of(first, BEA), BEA), :1] - source * 512
        row_at = jnp.concatenate([raw_rows, at] * 2, axis=0)
        rank = first + lax.broadcasted_iota(jnp.int32, (BEA, 1), 0)
        row_rank = jnp.concatenate([no_rank, rank] * 2, axis=0)
        allowed = jnp.concatenate([key_at <= row_at, beacon_at <= row_rank], axis=1)
        near = jnp.where(allowed, scores[:, :768], LOWEST)
        scores = jnp.concatenate([near, scores[:, 768:]], axis=1) if source else near
        kept = [r[tile, TOK:, :] for r in pieces] + [own_values]
        kept += [r[span_tile(e), TOK:, :] for e in range(source) for r in pieces]
        values = jnp.concatenate(kept, axis=0)
        old = m_in[tile, rows, :]
        new = jnp.maximum(old, jnp.max(scores, axis=1, keepdims=True))
        weights = jnp.exp2(scores - new[:, :1]).astype(BF16)
        mixed = jnp.dot(
            weights,
            jnp.concatenate([values, jnp.ones_like(values)], axis=1),
            preferred_element_type=F32,
        )
        factor = jnp.exp2(old - new)
        m_ref[tile, rows, :] = new
        l_ref[tile, rows, :] = l_in[tile, rows, :] * factor + mixed[:, HD:]
        a_ref[tile, rows, :] = a_in[tile, rows, :] * factor + mixed[:, :HD]


def attend_own_x(place, visible, q_ref, mine, other, m_ref, l_ref, a_ref, chosen, k_buf, v_buf):
    m_ref[...] = jnp.full(m_ref.shape, LOWEST, F32)
    l_ref[...] = jnp.zeros(l_ref.shape, F32)
    a_ref[...] = jnp.zeros(a_ref.shape, F32)
    count = list_visible(place, visible, (0,), chosen)
    run = functools.partial(over_tiles, q_ref, 0, m_ref, l_ref, a_ref)
    absorb_many(count, chosen, ((mine, other),), k_buf, v_buf, run)


def attend_prior(first, place, visible, q_ref, *rest):
    sources = tuple(zip(rest[:3], rest[3:6]))
    m_in, l_in, a_in, *outs = rest[6:-6]
    m_ref, l_ref, a_ref, chosen, k_buf, v_buf = rest[-6:]
    tiles = pl.ds(first, len(outs))
    m_ref[...] = m_in[tiles]
    l_ref[...] = l_in[tiles]
    a_ref[...] = a_in[tiles]
    count = list_visible(place, visible, (1, 3, 2), chosen)
    run = functools.partial(over_tiles, q_ref, first, m_ref, l_ref, a_ref)
    absorb_many(count, chosen, sources, k_buf, v_buf, run)
    for tile, out in enumerate(outs):
        out[...] = (a_ref[tile] / l_ref[tile]).astype(BF16)


def unpack_outputs(place, r0, r1, r2, r3, tok_ref, bea_ref):
    g = place[2] // 2
    for step, ref in enumerate((r0, r1, r2, r3)):
        dest = lax.rem(g + step, KVH)
        for h in range(GROUP):
            column = pl.multiple_of((dest * GROUP + h) * HD, HD)
            tok_ref[:, pl.ds(column, HD)] = ref[h * HEAD_ROWS : h * HEAD_ROWS + TOK, :]
            bea_ref[:, pl.ds(column, HD)] = ref[h * HEAD_ROWS + TOK : (h + 1) * HEAD_ROWS, :]


def on_device(q_tok, keys, values, beacon_q, beacon_k, beacon_v, beacon_pos, visible):
    place = jnp.stack([lax.axis_index(a) for a in CHIPS]).astype(jnp.int32)
    bpos = jnp.broadcast_to(beacon_pos[:, None], (256, HD))
    chunks = kernel_call(
        pack_tokens,
        "pack_tokens",
        [jax.ShapeDtypeStruct((TILE + 2 * TOK, HD), BF16)] * TILES,
        [SMEM] + [VMEM] * 4,
        byte_count=1000,
    )(place, q_tok, keys, values, beacon_q)
    got = [chunks[0]] + [
        lax.ppermute(chunks[step], CHIPS, to_head_group(step)) for step in range(1, TILES)
    ]
    to_send = kernel_call(
        pack_beacons,
        "pack_beacons",
        jax.ShapeDtypeStruct((NY * NZ, BEA, 2 * HD), BF16),
        [VMEM] * 2,
        byte_count=1000,
    )(beacon_k, beacon_v)
    arrived = lax.all_to_all(to_send, ("y", "z"), 0, 0, tiled=True)
    block0 = arrived.reshape(NY, HALF, 2 * HD)

    *got, _ = lax.optimization_barrier((*got, block0))
    asked = jnp.stack([piece[:TILE] for piece in got])
    kv_o = jnp.stack([piece[TILE:] for piece in got])
    block0c = lax.ppermute(block0, CHIPS, OTHER_CORE)

    state_shape = [jax.ShapeDtypeStruct((TILES, TILE, HD), F32)] * 3
    scratch = [
        pltpu.SMEM((NX * NY,), jnp.int32),
        pltpu.VMEM((6 * 2 * HALF, HD), BF16),
        pltpu.VMEM((6 * 2 * HALF, 2 * HD), BF16),
    ]
    state = kernel_call(
        attend_own_x,
        "attend_own_x",
        state_shape,
        [SMEM] * 2 + [VMEM] * 3,
        scratch,
        flops=1000,
        byte_count=1000,
    )(place, visible, asked, block0, block0c)
    kv_z = lax.ppermute(kv_o, CHIPS, OTHER_PARITY)
    kv_c = lax.ppermute(kv_o, CHIPS, OTHER_CORE)
    kv_z, _ = lax.optimization_barrier((kv_z, state[1]))
    kv_zc = lax.ppermute(kv_z, CHIPS, OTHER_CORE)
    state = kernel_call(
        attend_raw,
        "attend_raw",
        state_shape,
        [SMEM] + [VMEM] * 11,
        flops=1000,
        byte_count=1000,
    )(place, bpos, asked, kv_o, kv_c, kv_z, kv_zc, block0, block0c, *state)
    arriving = [lax.ppermute(block0, CHIPS, to_later_x(step)) for step in (1, 3, 2)]
    *arriving, _ = lax.optimization_barrier((*arriving, state[1]))
    crossed = [lax.ppermute(block, CHIPS, OTHER_CORE) for block in arriving]
    mixed = []
    for first, tiles in ((2, 2), (1, 1), (0, 1)):
        mixed = list(
            kernel_call(
                functools.partial(attend_prior, first),
                f"attend_prior_{first}",
                [jax.ShapeDtypeStruct((TILE, HD), BF16)] * tiles,
                [SMEM] * 2 + [VMEM] * 10,
                [pltpu.VMEM((tiles, TILE, HD), F32)] * 3 + scratch,
                flops=1000,
                byte_count=1000,
            )(place, visible, asked, *arriving, *crossed, *state)
        ) + mixed
    back = [mixed[0]] + [
        lax.ppermute(mixed[step], CHIPS, to_head_group(-step)) for step in range(1, TILES)
    ]
    return kernel_call(
        unpack_outputs,
        "unpack_outputs",
        [
            jax.ShapeDtypeStruct((TOK, QH * HD), BF16),
            jax.ShapeDtypeStruct((BEA, QH * HD), BF16),
        ],
        [SMEM] + [VMEM] * 4,
        byte_count=1000,
    )(place, *back)


def solution(mesh):
    chips = Mesh(mesh.devices.reshape(NX, NY, NZ, NC), CHIPS)
    rows = P(CHIPS, None)
    return jax.shard_map(
        on_device,
        mesh=chips,
        in_specs=(rows, rows, rows, rows, rows, rows, P(("x", "y")), P()),
        out_specs=(rows, rows),
        check_vma=False,
    )
```

```python
import functools

import jax
import jax.numpy as jnp
from jax import lax
from jax.experimental import pallas as pl
from jax.experimental.pallas import tpu as pltpu
from jax.sharding import Mesh, PartitionSpec as P

HD = 128
KVH = 4
QH = 16
GROUP = QH // KVH
NX, NY, NZ, NC = 4, 8, 8, 2
TOK = 128
BEA = 16
HEAD_ROWS = TOK + BEA
TILE = GROUP * HEAD_ROWS
TILES = 4
ROWS = TILES * TILE
HALF = 128
SCALE = HD**-0.5 * 1.4426950408889634
LOWEST = -1e30
CHIPS = ("x", "y", "z", "core")
CONTRACT_LAST = (((1,), (1,)), ((), ()))
VMEM = pl.BlockSpec(memory_space=pltpu.VMEM)
SMEM = pl.BlockSpec(memory_space=pltpu.SMEM)
BF16 = jnp.bfloat16
F32 = jnp.float32


def moves(target):
    pairs = []
    for x in range(NX):
        for y in range(NY):
            for z in range(NZ):
                for core in range(NC):
                    to = target(x, y, z, core)
                    if to is not None:
                        tx, ty, tz, tc = to
                        source = ((x * NY + y) * NZ + z) * NC + core
                        pairs.append((source, ((tx * NY + ty) * NZ + tz % NZ) * NC + tc))
    return pairs


def to_head_group(step):
    return moves(lambda x, y, z, core: (x, y, z + 2 * step, core))


def to_later_x(step):
    return moves(lambda x, y, z, core: (x + step, y, z, core) if x + step < NX else None)


OTHER_CORE = moves(lambda x, y, z, core: (x, y, z, 1 - core))
OTHER_PARITY = moves(lambda x, y, z, core: (x, y, z ^ 1, core))


def kernel_call(body, name, out_shape, in_specs, scratch=(), flops=0, byte_count=0):
    return pl.pallas_call(
        body,
        name=name,
        out_shape=out_shape,
        in_specs=in_specs,
        out_specs=jax.tree.map(lambda _: VMEM, out_shape),
        scratch_shapes=list(scratch),
        compiler_params=pltpu.CompilerParams(vmem_limit_bytes=20 * 2**20),
        cost_estimate=pl.CostEstimate(
            flops=flops, bytes_accessed=byte_count, transcendentals=0
        ),
    )


def pack_beacons(k_ref, v_ref, out_ref):
    for z in range(NZ):
        g = z // 2
        piece = jnp.concatenate(
            [k_ref[:, g * HD : (g + 1) * HD], v_ref[:, g * HD : (g + 1) * HD]], axis=1
        )
        for y in range(NY):
            out_ref[y * NZ + z] = piece


def pack_tokens(place, q_ref, k_ref, v_ref, bq_ref, *outs):
    g = place[2] // 2
    for step in range(TILES):
        dest = lax.rem(g + step, KVH)
        out = outs[step]
        for h in range(GROUP):
            column = pl.multiple_of((dest * GROUP + h) * HD, HD)
            out[h * HEAD_ROWS : h * HEAD_ROWS + TOK, :] = q_ref[:, pl.ds(column, HD)]
            out[h * HEAD_ROWS + TOK : (h + 1) * HEAD_ROWS, :] = bq_ref[:, pl.ds(column, HD)]
        column = pl.multiple_of(dest * HD, HD)
        out[TILE : TILE + TOK, :] = k_ref[:, pl.ds(column, HD)]
        out[TILE + TOK : TILE + 2 * TOK, :] = v_ref[:, pl.ds(column, HD)]


def absorb(state, rows, scores, values):
    m_ref, l_ref, a_ref = state
    old = m_ref[rows, :]
    new = jnp.maximum(old, jnp.max(scores, axis=1, keepdims=True))
    weights = jnp.exp2(scores - new[:, :1]).astype(BF16)
    mixed = jnp.dot(weights, values, preferred_element_type=F32)
    factor = jnp.exp2(old - new)
    m_ref[rows, :] = new
    l_ref[rows, :] = l_ref[rows, :] * factor + mixed[:, HD:]
    a_ref[rows, :] = a_ref[rows, :] * factor + mixed[:, :HD]


def score(asked, keys):
    return lax.dot_general(asked, keys, CONTRACT_LAST, preferred_element_type=F32) * SCALE


def list_visible(place, visible, shifts, chosen):
    my_span = place[0] * NY + place[1]
    count = jnp.int32(0)
    for block, shift in enumerate(shifts):
        first = lax.rem(place[0] + NX - shift, NX) * NY
        for y in range(NY):
            earlier = first + y
            usable = (earlier < my_span) & (visible[my_span, earlier] > 0)

            @pl.when(usable)
            def _():
                chosen[count] = block * NY + y

            count = count + usable.astype(jnp.int32)
    return count


def absorb_tile(asked, state, keys, values):
    both = [score(asked[rows, :], keys) for rows in HALVES]
    for rows, scores in zip(HALVES, both):
        absorb(state, rows, scores, values)


def absorb_block(first, size, count, chosen, sources, k_buf, v_buf, run):
    for j in range(size):
        rows = slice(j * 2 * HALF, (j + 1) * 2 * HALF)
        entry = chosen[jnp.minimum(first + j, count - 1)]
        real = first + j < count
        for index, refs in enumerate(sources):

            @pl.when(entry // NY == index)
            def _(refs=refs, rows=rows, entry=entry, real=real):
                span = lax.rem(entry, NY)
                k_buf[rows, :] = jnp.concatenate([r[span, :, :HD] for r in refs], axis=0)

                @pl.when(real)
                def _():
                    v_buf[rows, :HD] = jnp.concatenate([r[span, :, HD:] for r in refs], axis=0)
                    v_buf[rows, HD:] = jnp.ones((2 * HALF, HD), BF16)

                @pl.when(jnp.logical_not(real))
                def _():
                    v_buf[rows, :] = jnp.zeros((2 * HALF, 2 * HD), BF16)

    run(k_buf[: size * 2 * HALF, :], v_buf[: size * 2 * HALF, :])


def absorb_many(count, chosen, sources, k_buf, v_buf, run):
    left = lax.rem(count, 4)
    fold = (left > 0) & (left < 3) & (count > 4)
    blocks = jnp.where(fold, count // 4 - 1, (count + 3) // 4)

    def step(i, _):
        absorb_block(4 * i, 4, count, chosen, sources, k_buf, v_buf, run)
        return 0

    lax.fori_loop(0, blocks, step, 0)

    @pl.when(fold)
    def _():
        absorb_block(4 * blocks, 6, count, chosen, sources, k_buf, v_buf, run)


HALVES = (slice(0, TILE // 2), slice(TILE // 2, TILE))


def over_tiles(q_ref, first, m_ref, l_ref, a_ref, keys, values):
    def tile_step(tile, _):
        state = (m_ref.at[tile], l_ref.at[tile], a_ref.at[tile])
        absorb_tile(q_ref.at[first + tile], state, keys, values)
        return 0

    lax.fori_loop(0, m_ref.shape[0], tile_step, 0)


def attend_raw(
    place, bpos, q_ref, kv_o, kv_c, kv_z, kv_zc, mine, other, m_in, l_in, a_in, m_ref, l_ref, a_ref
):
    y, z, core = place[1], place[2], place[3]
    g, parity = z // 2, lax.rem(z, 2)
    pieces = (kv_o, kv_c, kv_z, kv_zc)
    here = parity * 256 + core * 128
    lane = lax.broadcasted_iota(jnp.int32, (1, 512), 1)
    combo = lane // 128
    key_at = ((parity ^ (combo // 2)) * 2 + (core ^ (combo % 2))) * 128 + lane % 128
    blane = lax.broadcasted_iota(jnp.int32, (1, 256), 1)
    brow = blane % 128
    beacon_at = (brow // BEA) * 32 + (core ^ (blane // 128)) * BEA + brow % BEA
    raw_rows = lax.broadcasted_iota(jnp.int32, (TOK, 1), 0) + here
    no_rank = jnp.full((TOK, 1), -1, jnp.int32)
    own_keys = jnp.concatenate([mine[y, :, :HD], other[y, :, :HD]], axis=0)
    own_values = jnp.concatenate([mine[y, :, HD:], other[y, :, HD:]], axis=0)

    def span_tile(source):
        return lax.rem(g - source + KVH, KVH)

    def ask(source, rows):
        tile = span_tile(source)
        kept = [r[tile, :TOK, :] for r in pieces] + [own_keys]
        kept += [r[span_tile(e), :TOK, :] for e in range(source) for r in pieces]
        return score(q_ref[tile, rows, :], jnp.concatenate(kept, axis=0))

    parts = [(source, rows) for source in (3, 2, 1, 0) for rows in HALVES]
    coming = ask(*parts[0])
    for index, (source, rows) in enumerate(parts):
        scores = coming
        if index + 1 < len(parts):
            coming = ask(*parts[index + 1])
        tile = span_tile(source)
        first = source * 64 + parity * 32 + core * BEA
        at = bpos[pl.ds(pl.multiple_of(first, BEA), BEA), :1] - source * 512
        row_at = jnp.concatenate([raw_rows, at] * 2, axis=0)
        rank = first + lax.broadcasted_iota(jnp.int32, (BEA, 1), 0)
        row_rank = jnp.concatenate([no_rank, rank] * 2, axis=0)
        allowed = jnp.concatenate([key_at <= row_at, beacon_at <= row_rank], axis=1)
        near = jnp.where(allowed, scores[:, :768], LOWEST)
        scores = jnp.concatenate([near, scores[:, 768:]], axis=1) if source else near
        kept = [r[tile, TOK:, :] for r in pieces] + [own_values]
        kept += [r[span_tile(e), TOK:, :] for e in range(source) for r in pieces]
        values = jnp.concatenate(kept, axis=0)
        old = m_in[tile, rows, :]
        new = jnp.maximum(old, jnp.max(scores, axis=1, keepdims=True))
        weights = jnp.exp2(scores - new[:, :1]).astype(BF16)
        mixed = jnp.dot(
            weights,
            jnp.concatenate([values, jnp.ones_like(values)], axis=1),
            preferred_element_type=F32,
        )
        factor = jnp.exp2(old - new)
        m_ref[tile, rows, :] = new
        l_ref[tile, rows, :] = l_in[tile, rows, :] * factor + mixed[:, HD:]
        a_ref[tile, rows, :] = a_in[tile, rows, :] * factor + mixed[:, :HD]


def attend_own_x(place, visible, q_ref, mine, other, m_ref, l_ref, a_ref, chosen, k_buf, v_buf):
    m_ref[...] = jnp.full(m_ref.shape, LOWEST, F32)
    l_ref[...] = jnp.zeros(l_ref.shape, F32)
    a_ref[...] = jnp.zeros(a_ref.shape, F32)
    count = list_visible(place, visible, (0,), chosen)
    run = functools.partial(over_tiles, q_ref, 0, m_ref, l_ref, a_ref)
    absorb_many(count, chosen, ((mine, other),), k_buf, v_buf, run)


def attend_prior(first, place, visible, q_ref, *rest):
    sources = tuple(zip(rest[:3], rest[3:6]))
    m_in, l_in, a_in, *outs = rest[6:-6]
    m_ref, l_ref, a_ref, chosen, k_buf, v_buf = rest[-6:]
    tiles = pl.ds(first, len(outs))
    m_ref[...] = m_in[tiles]
    l_ref[...] = l_in[tiles]
    a_ref[...] = a_in[tiles]
    count = list_visible(place, visible, (1, 3, 2), chosen)
    run = functools.partial(over_tiles, q_ref, first, m_ref, l_ref, a_ref)
    absorb_many(count, chosen, sources, k_buf, v_buf, run)
    for tile, out in enumerate(outs):
        out[...] = (a_ref[tile] / l_ref[tile]).astype(BF16)


def unpack_outputs(place, r0, r1, r2, r3, tok_ref, bea_ref):
    g = place[2] // 2
    for step, ref in enumerate((r0, r1, r2, r3)):
        dest = lax.rem(g + step, KVH)
        for h in range(GROUP):
            column = pl.multiple_of((dest * GROUP + h) * HD, HD)
            tok_ref[:, pl.ds(column, HD)] = ref[h * HEAD_ROWS : h * HEAD_ROWS + TOK, :]
            bea_ref[:, pl.ds(column, HD)] = ref[h * HEAD_ROWS + TOK : (h + 1) * HEAD_ROWS, :]


def on_device(q_tok, keys, values, beacon_q, beacon_k, beacon_v, beacon_pos, visible):
    place = jnp.stack([lax.axis_index(a) for a in CHIPS]).astype(jnp.int32)
    bpos = jnp.broadcast_to(beacon_pos[:, None], (256, HD))
    chunks = kernel_call(
        pack_tokens,
        "pack_tokens",
        [jax.ShapeDtypeStruct((TILE + 2 * TOK, HD), BF16)] * TILES,
        [SMEM] + [VMEM] * 4,
        byte_count=1000,
    )(place, q_tok, keys, values, beacon_q)
    got = [chunks[0]] + [
        lax.ppermute(chunks[step], CHIPS, to_head_group(step)) for step in range(1, TILES)
    ]
    to_send = kernel_call(
        pack_beacons,
        "pack_beacons",
        jax.ShapeDtypeStruct((NY * NZ, BEA, 2 * HD), BF16),
        [VMEM] * 2,
        byte_count=1000,
    )(beacon_k, beacon_v)
    arrived = lax.all_to_all(to_send, ("y", "z"), 0, 0, tiled=True)
    block0 = arrived.reshape(NY, HALF, 2 * HD)

    *got, _ = lax.optimization_barrier((*got, block0))
    asked = jnp.stack([piece[:TILE] for piece in got])
    kv_o = jnp.stack([piece[TILE:] for piece in got])
    block0c = lax.ppermute(block0, CHIPS, OTHER_CORE)

    state_shape = [jax.ShapeDtypeStruct((TILES, TILE, HD), F32)] * 3
    scratch = [
        pltpu.SMEM((NX * NY,), jnp.int32),
        pltpu.VMEM((6 * 2 * HALF, HD), BF16),
        pltpu.VMEM((6 * 2 * HALF, 2 * HD), BF16),
    ]
    state = kernel_call(
        attend_own_x,
        "attend_own_x",
        state_shape,
        [SMEM] * 2 + [VMEM] * 3,
        scratch,
        flops=1000,
        byte_count=1000,
    )(place, visible, asked, block0, block0c)
    kv_z = lax.ppermute(kv_o, CHIPS, OTHER_PARITY)
    kv_c = lax.ppermute(kv_o, CHIPS, OTHER_CORE)
    kv_z, _ = lax.optimization_barrier((kv_z, state[1]))
    kv_zc = lax.ppermute(kv_z, CHIPS, OTHER_CORE)
    state = kernel_call(
        attend_raw,
        "attend_raw",
        state_shape,
        [SMEM] + [VMEM] * 11,
        flops=1000,
        byte_count=1000,
    )(place, bpos, asked, kv_o, kv_c, kv_z, kv_zc, block0, block0c, *state)
    near = [lax.ppermute(block0, CHIPS, to_later_x(step)) for step in (1, 3)]
    *near, _ = lax.optimization_barrier((*near, kv_z))
    far = lax.ppermute(block0, CHIPS, to_later_x(2))
    far, _ = lax.optimization_barrier((far, state[1]))
    arriving = [*near, far]
    crossed = [lax.ppermute(block, CHIPS, OTHER_CORE) for block in arriving]
    mixed = []
    for first, tiles in ((1, 3), (0, 1)):
        mixed = list(
            kernel_call(
                functools.partial(attend_prior, first),
                f"attend_prior_{first}",
                [jax.ShapeDtypeStruct((TILE, HD), BF16)] * tiles,
                [SMEM] * 2 + [VMEM] * 10,
                [pltpu.VMEM((tiles, TILE, HD), F32)] * 3 + scratch,
                flops=1000,
                byte_count=1000,
            )(place, visible, asked, *arriving, *crossed, *state)
        ) + mixed
    back = [mixed[0]] + [
        lax.ppermute(mixed[step], CHIPS, to_head_group(-step)) for step in range(1, TILES)
    ]
    return kernel_call(
        unpack_outputs,
        "unpack_outputs",
        [
            jax.ShapeDtypeStruct((TOK, QH * HD), BF16),
            jax.ShapeDtypeStruct((BEA, QH * HD), BF16),
        ],
        [SMEM] + [VMEM] * 4,
        byte_count=1000,
    )(place, *back)


def solution(mesh):
    chips = Mesh(mesh.devices.reshape(NX, NY, NZ, NC), CHIPS)
    rows = P(CHIPS, None)
    return jax.shard_map(
        on_device,
        mesh=chips,
        in_specs=(rows, rows, rows, rows, rows, rows, P(("x", "y")), P()),
        out_specs=(rows, rows),
        check_vma=False,
    )
```
